256 devices in a mesh: ctx: 64 (over z, x, core), kvh: 4 (over y).
Axes of the slice: x: 4, y: 4, z: 8, core: 2. Of those that a mesh axis runs over, the one named last changes fastest.
Arguments:
- hidden: bfloat16 [8192, 4096], P('ctx', 'kvh'), may hold values from -16 to 16
- query_weight: bfloat16 [4096, 2048], P('ctx', 'kvh'), may hold values from -0.09375 to 0.09375
- probe_vector: bfloat16 [4096, 2048], P('ctx', 'kvh'), may hold values from -6 to 6
- key_rows: bfloat16 [8192, 512], P('ctx', 'kvh'), may hold values from -6 to 6
- value_rows: bfloat16 [8192, 512], P('ctx', 'kvh'), may hold values from -6 to 6
- upstream: bfloat16 [8192, 2048], P('ctx', 'kvh'), may hold values from -1.25 to 1.25
- lengths: int32 [16], replicated, may hold values from 1 to 2048, 8192 in all
- block_order: int32 [128], replicated, may hold values from 0 to 127, each once
Outputs:
- curvature: float32 [4096, 2048], P('ctx', 'kvh')
The draws below stay inside these ranges and needn't reach their ends.
Inputs may be any that keep to these rules, and one draw needn't show every extreme that they name: The lengths sum to 8192. `block_order`: each block number appears once.
All inputs are finite; a program needn't handle non-finite values.
Results may differ from the reference program's by a relative error of at most 0.01.
Values may be sent and summed in bfloat16 or wider, within the bound.
No kernel may reach another device: no remote copies, remote signals or barrier semaphores. Data moves between devices by JAX's collectives and lax.ppermute only.
A program may use at most 64 MiB of HBM per device.

```python
import math
import jax
import jax.numpy as jnp
import numpy as np
from jax import lax

D = 4096
H = 16
KVH = 4
HD = 128
TOKENS = 8192
BLK = 64
NBLK = 128
NDOC = 16
MOST = 2048


def raised(values, stream_key, source, target, shards_of, factor):
    owner, partner = [(jnp.arange(values.shape[dim]) // (values.shape[dim] // shards_of)).reshape([-1 if axis == dim else 1 for axis in range(values.ndim)]) for dim in (source, target)]
    chosen = jax.random.permutation(stream_key, shards_of)[partner]
    strong = (owner == chosen) | (owner == (partner + shards_of // 2) % shards_of)
    return jnp.where(strong, factor * values, values)


def level_of(own_key, shape, cuts, least, largest):
    def one(dim, parts):
        heights = jax.random.uniform(jax.random.fold_in(jax.random.fold_in(own_key, 6), dim), (parts,), jnp.float32, least / len(cuts), largest / len(cuts))
        return jnp.repeat(jnp.exp(heights), shape[dim] // parts).reshape((-1,) + (1,) * (len(shape) - dim - 1))

    gain = one(*cuts[0])
    for cut in cuts[1:]:
        gain = gain * one(*cut)
    return gain


def split_up(number_of, total, bound, lean):
    weights = [(1 << 20) // math.isqrt(standing ** lean) + 1 for standing in range(2, number_of + 1)]
    rest, counts = total - bound - (number_of - 1), [1] * (number_of - 1)
    while rest > 0:
        movable = [i for i in range(number_of - 1) if counts[i] < bound]
        pool, budget = sum([weights[i] for i in movable]), rest
        for i in movable:
            addition = min(bound - counts[i], max(1, budget * weights[i] // pool), rest)
            counts[i] = counts[i] + addition
            rest = rest - addition
    return np.array([bound] + counts)


def uneven(own_key, number_of, total, most, lean):
    if number_of == 2:
        one = jax.random.randint(own_key, (), max(1, total - most), min(most, total - 1) + 1)
        return jnp.stack([one, total - one])
    tallies = jnp.asarray(split_up(number_of, total, most, lean), jnp.int32)
    pairs = (number_of - 1) // 2
    donor, taker = tallies[1:1 + 2 * pairs:2], tallies[2:2 + 2 * pairs:2]
    slack = jnp.minimum(donor - 1, most - taker)
    passed = jax.random.randint(jax.random.fold_in(own_key, 1), (pairs,), 0, 1 << 20) % (slack + 1)
    tallies = tallies.at[1:1 + 2 * pairs:2].set(donor - passed).at[2:2 + 2 * pairs:2].set(taker + passed)
    return tallies[jax.random.permutation(jax.random.fold_in(own_key, 2), number_of)]


def centred(own_key, shape, width, reach, shards=(), kind=jnp.bfloat16):
    result = jax.random.normal(own_key, shape, jnp.float32) * width
    if len(shards) > 0:
        result = level_of(own_key, shape, shards, -0.22, 0.18) * result
    return jnp.clip(result, min=-reach, max=reach).astype(kind)


def heavy_noise(key, dims, deviation, most, pieces, heavy, kind=jnp.bfloat16):
    drawn = deviation * jax.random.normal(key, dims, jnp.float32)
    if pieces:
        drawn = drawn * level_of(key, dims, pieces, -0.22, 0.18)
    return jnp.clip(raised(drawn, jax.random.fold_in(key, 3), *heavy), -most, most).astype(kind)


def setup_inputs(seed: int = 0) -> dict:
    seeds = jax.random.split(jax.random.key(seed), 9)
    hidden = heavy_noise(seeds[0], (TOKENS, D), 1.0, 16.0, ((0, 64), (1, 4)), (0, 1, 64, 4.0))
    query_weight = centred(seeds[1], (D, H * HD), D ** -0.5, 0.09375, ((0, 64), (1, 4)))
    probe_vector = centred(seeds[2], (D, H * HD), 1.0, 6.0, ((0, 64), (1, 4)))
    key_rows = centred(seeds[3], (TOKENS, KVH * HD), 1.0, 6.0, ((0, 64), (1, 4)))
    value_rows = centred(seeds[4], (TOKENS, KVH * HD), 1.0, 6.0, ((0, 64), (1, 4)))
    upstream = centred(seeds[5], (TOKENS, H * HD), 0.0884, 1.25, ((0, 64), (1, 4)))
    lengths = uneven(seeds[6], NDOC, TOKENS, MOST, 2).astype(jnp.int32)
    block_order = jax.random.permutation(seeds[7], NBLK).astype(jnp.int32)
    return dict(hidden=hidden, query_weight=query_weight, probe_vector=probe_vector, key_rows=key_rows, value_rows=value_rows, upstream=upstream, lengths=lengths, block_order=block_order)


def reference(hidden, query_weight, probe_vector, key_rows, value_rows, upstream, lengths, block_order):
    score_scale = 1.0 / math.sqrt(HD)
    query_all = jnp.dot(hidden, query_weight, preferred_element_type=jnp.float32).astype(jnp.bfloat16)
    tangent_all = jnp.dot(hidden, probe_vector, preferred_element_type=jnp.float32).astype(jnp.bfloat16)
    layout = jnp.arange(TOKENS, dtype=jnp.int32)
    position = block_order[layout // BLK] * BLK + layout % BLK
    doc_ends = jnp.cumsum(lengths).astype(jnp.int32)
    document = lax.optimization_barrier(jnp.sum((position[:, None] >= doc_ends[None, :]).astype(jnp.int32), axis=1))
    group_size = H // KVH
    block_count = max(1, TOKENS // 1024)
    block_size = TOKENS // block_count

    def per_head(head_index):
        kv_index = head_index // group_size
        query_head = lax.dynamic_slice_in_dim(query_all, head_index * HD, HD, 1)
        tangent_head = lax.dynamic_slice_in_dim(tangent_all, head_index * HD, HD, 1)
        upstream_head = lax.dynamic_slice_in_dim(upstream, head_index * HD, HD, 1)
        key_head = lax.dynamic_slice_in_dim(key_rows, kv_index * HD, HD, 1)
        value_head = lax.dynamic_slice_in_dim(value_rows, kv_index * HD, HD, 1)

        def per_block(block_index):
            first_row = block_index * block_size
            query_block = lax.dynamic_slice_in_dim(query_head, first_row, block_size, 0)
            tangent_block = lax.dynamic_slice_in_dim(tangent_head, first_row, block_size, 0)
            upstream_block = lax.dynamic_slice_in_dim(upstream_head, first_row, block_size, 0)
            position_block = lax.dynamic_slice_in_dim(position, first_row, block_size, 0)
            document_block = lax.dynamic_slice_in_dim(document, first_row, block_size, 0)
            scores = jnp.dot(query_block, key_head.T, preferred_element_type=jnp.float32) * score_scale
            tangent_scores = jnp.dot(tangent_block, key_head.T, preferred_element_type=jnp.float32) * score_scale
            value_match = jnp.dot(upstream_block, value_head.T, preferred_element_type=jnp.float32)
            allowed = (document_block[:, None] == document[None, :]) & (position[None, :] <= position_block[:, None])
            exp_scores = jnp.where(allowed, jnp.exp(scores), 0.0)
            weight_sum = lax.optimization_barrier(jnp.sum(exp_scores, axis=1))
            value_sum = lax.optimization_barrier(jnp.sum(exp_scores * value_match, axis=1))
            tangent_sum = lax.optimization_barrier(jnp.sum(exp_scores * tangent_scores, axis=1))
            joint_sum = lax.optimization_barrier(jnp.sum(exp_scores * value_match * tangent_scores, axis=1))
            value_mean = value_sum / weight_sum
            tangent_mean = tangent_sum / weight_sum
            value_drift = joint_sum / weight_sum - tangent_mean * value_mean
            weight = (exp_scores / weight_sum[:, None] * ((tangent_scores - tangent_mean[:, None]) * (value_match - value_mean[:, None]) - value_drift[:, None])).astype(jnp.bfloat16)
            return jnp.dot(weight, key_head, preferred_element_type=jnp.float32) * score_scale
        return lax.map(per_block, jnp.arange(block_count, dtype=jnp.int32))
    blocks = lax.map(per_head, jnp.arange(H, dtype=jnp.int32))
    second_order = blocks.reshape(H, TOKENS, HD).transpose(1, 0, 2).reshape(TOKENS, H * HD).astype(jnp.bfloat16)
    return jnp.dot(hidden.T, second_order, preferred_element_type=jnp.float32)
```

```python
import functools
import math

import jax
import jax.numpy as jnp
from jax import lax
from jax.experimental import pallas as pl
from jax.experimental.pallas import tpu as pltpu
from jax.sharding import Mesh, PartitionSpec as P

HD = 128
BLK = 64
NDOC = 16
CHUNK_BLOCKS = 8
CHUNK = CHUNK_BLOCKS * BLK
MAX_CHUNKS = 5
SCALE = 1.0 / math.sqrt(HD)
LOG2E = 1.4426950408889634
TOKENS = 8192
D = 4096
BF16 = jnp.bfloat16
F32 = jnp.float32


def fused_kernel(
    where_ref,
    order_ref,
    lengths_ref,
    h1_own,
    h1_right,
    h1_left,
    h1_far_a,
    h1_far_b,
    h2_own,
    h2_right,
    h2_left,
    h2_far_a,
    h2_far_b,
    packed_own,
    packed_other,
    upstream_ref,
    keep_ref,
    send_ref,
    hid,
    weights,
    keys_values,
    query_tangent,
    second_t,
    exp_buf,
    tan_buf,
    val_buf,
    ends,
    sem_h,
    sem_w,
    sem_kv,
):
    z, x, c, y = where_ref[0], where_ref[1], where_ref[2], where_ref[3]

    for dx in range(4):
        xx = lax.rem(x - dx + 4, 4)
        for src, cc in ((packed_own, c), (packed_other, 1 - c)):
            row = pl.multiple_of((xx * 2 + cc) * 64, 64)
            pltpu.make_async_copy(
                src.at[:, pl.ds(dx * 192, 64), :], weights.at[:, pl.ds(row, 64), :], sem_w
            ).start()

    h1_pieces = []
    for dx, src in ((0, h1_own), (1, h1_right), (3, h1_left)):
        h1_pieces += [(dx, dy, src.at[dy]) for dy in range(4)]
    h1_pieces += [(2, 0, h1_far_a.at[0]), (2, 1, h1_far_a.at[1])]
    h1_pieces += [(2, 2, h1_far_b.at[0]), (2, 3, h1_far_b.at[1])]
    for dx, dy, src in h1_pieces:
        group = lax.rem(y - dy + 4, 4) * 2
        pltpu.make_async_copy(src, hid.at[group, pl.ds(dx * 128, 128), :], sem_h).start()
    for dy, row, rows, src in (
        (0, 0, 512, h2_own),
        (1, 0, 512, h2_right),
        (3, 0, 512, h2_left),
        (2, 0, 256, h2_far_a),
        (2, 256, 256, h2_far_b),
    ):
        group = lax.rem(y - dy + 4, 4) * 2 + 1
        pltpu.make_async_copy(src, hid.at[group, pl.ds(row, rows), :], sem_h).start()

    def place(i, carry):
        zz = i // 4
        dx = lax.rem(i, 4)
        xx = lax.rem(x - dx + 4, 4)
        for src, cc in ((packed_own, c), (packed_other, 1 - c)):
            block = ((zz * 4 + xx) * 2 + cc) * 2
            for b in range(2):
                target = pl.multiple_of(order_ref[block + b] * BLK, BLK)
                row = pl.multiple_of(dx * 192 + 64 + b * 64, 64)
                pltpu.make_async_copy(
                    src.at[zz, pl.ds(row, 64), :], keys_values.at[pl.ds(target, BLK), :], sem_kv
                ).start()
        return carry

    lax.fori_loop(0, 32, place, 0)
    keys_values[pl.ds(TOKENS, CHUNK), :] = jnp.zeros((CHUNK, 256), BF16)

    total = jnp.int32(0)
    for d in range(NDOC):
        total = total + lengths_ref[d]
        ends[d] = total

    pltpu.make_async_copy(weights, weights, sem_w).wait()
    pltpu.make_async_copy(hid, hid, sem_h).wait()

    acc = jnp.zeros((512, 256), F32)
    for g in range(8):
        acc = acc + jnp.dot(hid[g], weights[g], preferred_element_type=F32)
    projected = acc.astype(BF16)
    for rb in range(8):
        query_tangent[rb, 0:64, :] = projected[rb * 64 : rb * 64 + 64, 0:128]
        query_tangent[rb, 64:128, :] = projected[rb * 64 : rb * 64 + 64, 128:256]

    whole = keys_values.at[pl.ds(0, TOKENS), :]
    pltpu.make_async_copy(whole, whole, sem_kv).wait()

    def row_block(rb, carry):
        dx = rb // 2
        xx = lax.rem(x - dx + 4, 4)
        p = order_ref[((z * 4 + xx) * 2 + c) * 2 + lax.rem(rb, 2)]
        first_start = jnp.int32(0)
        pos = p * BLK + lax.broadcasted_iota(jnp.int32, (BLK, 1), 0)
        start = jnp.zeros((BLK, 1), jnp.int32)
        for d in range(NDOC):
            end = ends[d]
            first_start = jnp.where(end <= p * BLK, end, first_start)
            start = jnp.where(end <= pos, end, start)
        kb0 = first_start // BLK
        chunks = (p - kb0 + CHUNK_BLOCKS) // CHUNK_BLOCKS
        qt = query_tangent[rb]
        up = upstream_ref[rb]

        def first_pass(j, sums):
            k0 = pl.multiple_of((kb0 + j * CHUNK_BLOCKS) * BLK, BLK)
            kv = keys_values[pl.ds(k0, CHUNK), :]
            st = lax.dot_general(
                qt, kv[:, 0:128], (((1,), (1,)), ((), ())), preferred_element_type=F32
            )
            v = lax.dot_general(
                up, kv[:, 128:256], (((1,), (1,)), ((), ())), preferred_element_type=F32
            )
            s, t = st[0:64], st[64:128]
            key_pos = k0 + lax.broadcasted_iota(jnp.int32, (BLK, CHUNK), 1)
            allowed = (key_pos >= start) & (key_pos <= pos)
            e = jnp.where(allowed, jnp.exp2(s * (SCALE * LOG2E)), 0.0)
            exp_buf[j] = e
            tan_buf[j] = t
            val_buf[j] = v
            ev = e * v
            et = e * t
            evt = ev * t

            def lanes(a):
                out = a[:, 0:128]
                for i in range(1, CHUNK // 128):
                    out = out + a[:, i * 128 : (i + 1) * 128]
                return out

            return (
                sums[0] + lanes(e),
                sums[1] + lanes(ev),
                sums[2] + lanes(et),
                sums[3] + lanes(evt),
            )

        zero = jnp.zeros((BLK, 128), F32)
        sums = lax.fori_loop(0, chunks, first_pass, (zero, zero, zero, zero))
        weight_sum, value_sum, tangent_sum, joint_sum = [
            jnp.sum(a, axis=1, keepdims=True) for a in sums
        ]
        inverse = 1.0 / weight_sum
        value_mean = value_sum * inverse
        tangent_mean = tangent_sum * inverse
        drift = joint_sum * inverse - tangent_mean * value_mean

        def second_pass(j, total):
            k0 = pl.multiple_of((kb0 + j * CHUNK_BLOCKS) * BLK, BLK)
            keys = keys_values[pl.ds(k0, CHUNK), 0:128]
            w = (exp_buf[j] * inverse) * (
                (tan_buf[j] - tangent_mean) * (val_buf[j] - value_mean) - drift
            )
            return total + jnp.dot(w.astype(BF16), keys, preferred_element_type=F32)

        so = lax.fori_loop(0, chunks, second_pass, zero)
        second_t[pl.ds(pl.multiple_of(rb * 64, 64), 64), :] = so * (SCALE * SCALE)
        return carry

    lax.fori_loop(0, 8, row_block, 0)

    so_t = second_t[...].T.astype(BF16)
    for g in range(8):
        out = jnp.dot(so_t, hid[g], preferred_element_type=F32).T
        out = out.reshape(4, 2, 64, 128)
        rows = pl.ds(g * 256, 256)
        keep_ref[rows, :] = jnp.where(c == 0, out[:, 0], out[:, 1]).reshape(256, 128)
        send_ref[rows, :] = (
            jnp.where(c == 0, out[:, 1], out[:, 0]).reshape(256, 128).astype(BF16)
        )


def fused(scalars, pieces, interpret=False):
    any_spec = pl.BlockSpec(memory_space=pl.ANY)
    smem = pl.BlockSpec(memory_space=pltpu.SMEM)
    vmem = pl.BlockSpec(memory_space=pltpu.VMEM)
    return pl.pallas_call(
        fused_kernel,
        out_shape=(
            jax.ShapeDtypeStruct((2048, 128), F32),
            jax.ShapeDtypeStruct((2048, 128), BF16),
        ),
        in_specs=[smem] * 3 + [any_spec] * 12 + [vmem],
        out_specs=(vmem, vmem),
        scratch_shapes=[
            pltpu.VMEM((8, 512, 512), BF16),
            pltpu.VMEM((8, 512, 256), BF16),
            pltpu.VMEM((TOKENS + CHUNK, 256), BF16),
            pltpu.VMEM((8, 128, 128), BF16),
            pltpu.VMEM((512, 128), F32),
            pltpu.VMEM((MAX_CHUNKS, BLK, CHUNK), F32),
            pltpu.VMEM((MAX_CHUNKS, BLK, CHUNK), F32),
            pltpu.VMEM((MAX_CHUNKS, BLK, CHUNK), F32),
            pltpu.SMEM((NDOC,), jnp.int32),
            pltpu.SemaphoreType.DMA,
            pltpu.SemaphoreType.DMA,
            pltpu.SemaphoreType.DMA,
        ],
        compiler_params=pltpu.CompilerParams(vmem_limit_bytes=40 * 1024 * 1024),
        cost_estimate=pl.CostEstimate(
            flops=6_000_000_000, bytes_accessed=14_000_000, transcendentals=1_000_000
        ),
        interpret=interpret,
    )(*scalars, *pieces)


def shift(value, axis, size, step):
    return lax.ppermute(value, axis, [(i, (i + step) % size) for i in range(size)])


def gather_four(value, axis):
    return [value] + [shift(value, axis, 4, s) for s in (1, 2, 3)]


def ring_four(stack, axis):
    right = shift(stack, axis, 4, 1)
    left = shift(stack, axis, 4, 3)
    half = stack.shape[0] // 2
    far_a = shift(right[:half], axis, 4, 1)
    far_b = shift(left[half:], axis, 4, 3)
    return [stack, right, left, far_a, far_b]


def per_device(
    hidden, query_weight, probe_vector, key_rows, value_rows, upstream, lengths, block_order
):
    z = lax.axis_index("z")
    x = lax.axis_index("x")
    c = lax.axis_index("c")
    y = lax.axis_index("kvh")

    def head_slice(array, dx):
        head = lax.rem(x + dx, 4)
        return lax.dynamic_slice_in_dim(array, head * HD, HD, 1)

    keys_values = jnp.concatenate([key_rows, value_rows], axis=1)

    def pack(dx):
        both = jnp.concatenate([head_slice(query_weight, dx), head_slice(probe_vector, dx)], axis=1)
        return jnp.concatenate([both, keys_values], axis=0)

    packs = [pack(0)] + [shift(pack(dx), "x", 4, dx) for dx in (1, 2, 3)]
    packed_own = lax.all_gather(jnp.concatenate(packs, axis=0), "z", axis=0, tiled=True)

    first, second = hidden[:, :512], hidden[:, 512:]
    stack_1 = jnp.stack(gather_four(first, "kvh"))
    sent = [jnp.concatenate([second, head_slice(upstream, dx)], axis=1) for dx in range(4)]
    sent = [sent[0]] + [shift(sent[dx], "x", 4, dx) for dx in (1, 2, 3)]
    stack_2 = jnp.concatenate([m[:, :512] for m in sent], axis=0)
    upstream_rows = jnp.concatenate([m[:, 512:] for m in sent], axis=0).reshape(8, 64, 128)
    pieces_1 = ring_four(stack_1, "x")
    pieces_2 = ring_four(stack_2, "kvh")

    packed_own, *pieces = lax.optimization_barrier((packed_own, *pieces_1, *pieces_2))
    packed_other = shift(packed_own, "c", 2, 1)

    where = jnp.stack([z, x, c, y]).astype(jnp.int32)
    keep, send = fused(
        (where, block_order, lengths),
        (
            *pieces,
            packed_own.reshape(8, 768, 256),
            packed_other.reshape(8, 768, 256),
            upstream_rows,
        ),
    )
    received = shift(send, "c", 2, 1)
    partial = (keep + received.astype(F32)).astype(BF16)
    shares = lax.all_to_all(partial, ("z", "x"), 0, 0, tiled=True)
    summed = jnp.sum(shares.reshape(8, 4, 64, 128).astype(F32), axis=0)
    return summed.transpose(1, 0, 2).reshape(64, 512)


def solution(mesh):
    fine = Mesh(mesh.devices.reshape(8, 4, 2, 4), ("z", "x", "c", "kvh"))
    ctx = ("z", "x", "c")
    split = P(ctx, "kvh")
    return jax.shard_map(
        per_device,
        mesh=fine,
        in_specs=(split,) * 6 + (P(), P()),
        out_specs=split,
        check_vma=False,
    )
```

```python
import math

import jax
import jax.numpy as jnp
from jax import lax
from jax.experimental import pallas as pl
from jax.experimental.pallas import tpu as pltpu
from jax.sharding import Mesh, PartitionSpec as P

HD = 128
BLK = 64
NDOC = 16
CHUNK = 512
LANES = 128
ROW_BLOCKS = 8
MOST_EXTRA = ROW_BLOCKS * 4
SCALE = 1.0 / math.sqrt(HD)
LOG2E = 1.4426950408889634
TOKENS = 8192
BF16 = jnp.bfloat16
F32 = jnp.float32
I32 = jnp.int32


def prepare_kernel(
    where_ref,
    hidden_hbm,
    query_hbm,
    probe_hbm,
    key_hbm,
    value_hbm,
    upstream_hbm,
    pack0_ref,
    pack1_ref,
    pack2_ref,
    pack3_ref,
    keep_ref,
    send_ref,
    hidden_ref,
    query_ref,
    probe_ref,
    key_ref,
    value_ref,
    upstream_ref,
    sems,
):
    x, c = where_ref[1], where_ref[2]
    copies = [
        pltpu.make_async_copy(src, dst, sems.at[i])
        for i, (src, dst) in enumerate(
            (
                (query_hbm, query_ref),
                (probe_hbm, probe_ref),
                (key_hbm, key_ref),
                (value_hbm, value_ref),
                (upstream_hbm, upstream_ref),
                (hidden_hbm, hidden_ref),
            )
        )
    ]
    for copy in copies:
        copy.start()
    for copy in copies[:5]:
        copy.wait()
    for dx, pack in enumerate((pack0_ref, pack1_ref, pack2_ref, pack3_ref)):
        columns = pl.ds(pl.multiple_of(lax.rem(x + dx, 4) * HD, HD), HD)
        pack[0:64, 0:128] = query_ref[:, columns]
        pack[0:64, 128:256] = probe_ref[:, columns]
        pack[64:192, 0:128] = key_ref[...]
        pack[64:192, 128:256] = value_ref[...]
        pack[192:256, 0:128] = upstream_ref[0:64, columns]
        pack[192:256, 128:256] = upstream_ref[64:128, columns]
    copies[5].wait()
    low = lax.broadcasted_iota(I32, (128, 128), 1) < 64
    for k in range(4):
        a = hidden_ref[:, 256 * k : 256 * k + 128].astype(F32)
        b = hidden_ref[:, 256 * k + 128 : 256 * k + 256].astype(F32)
        first = jnp.where(low, a, pltpu.roll(b, 64, 1))
        second = jnp.where(low, pltpu.roll(a, 64, 1), b)
        cut = slice(128 * k, 128 * k + 128)
        keep_ref[:, cut] = jnp.where(c == 0, first, second).astype(BF16)
        send_ref[:, cut] = jnp.where(c == 0, second, first).astype(BF16)


def hidden_piece(refs, r, s):
    stack, right, left, far_a, far_b = refs
    if r == 2:
        return far_a[s] if s < 2 else far_b[s - 2]
    return (stack, right, None, left)[r][s]


def project_kernel(*refs):
    where_ref, hidden = refs[0], refs[1:6]
    packs, far_r, far_l = refs[6:13], refs[13], refs[14]
    keep_ref, send_ref, weights, total = refs[15:]
    z, x, c, y = where_ref[0], where_ref[1], where_ref[2], where_ref[3]

    def place(pack, dz, places=(0, 1, 2, 3)):
        for i, dx in enumerate(places):
            weights[lax.rem(z - dz + 8, 8), lax.rem(x - dx + 4, 4)] = pack[
                i * 192 : i * 192 + 64, :
            ]

    for pack, dz in zip(packs, (0, 1, 7, 2, 6, 3, 5)):
        place(pack, dz)
    place(far_r, 4, (0, 1))
    place(far_l, 4, (2, 3))

    total[...] = jnp.zeros((4, 256, 256), F32)
    for r in range(4):
        for s in range(4):
            dx = jnp.where(c == 0, r, s)
            dy = jnp.where(c == 0, s, r)
            group = lax.rem(y - dy + 4, 4)
            w = weights[pl.ds(group * 2, 2)].reshape(512, 256)
            total[dx] += jnp.dot(hidden_piece(hidden, r, s), w, preferred_element_type=F32)
    keep_ref[...] = total[:, 0:128, :]
    send_ref[...] = total[:, 128:256, :]


def attend_kernel(*refs):
    where_ref, order_ref, lengths_ref, qt_keep, qt_received = refs[:5]
    packs, far_r, far_l = refs[5:12], refs[12], refs[13]
    swap_a, swap_b, swap_c = refs[14:17]
    upstream_ref, second_ref = refs[17:19]
    (
        keys_values,
        query_tangent,
        starts,
        exp_buf,
        tan_buf,
        val_buf,
        sums,
        stats,
        second,
        ends,
        extra_block,
        extra_row,
    ) = refs[19:]
    z, x, c = where_ref[0], where_ref[1], where_ref[2]

    keys_values[0:CHUNK, :] = jnp.zeros((CHUNK, 256), BF16)

    def place(src, first_row, step, dz, cc, places=(0, 1, 2, 3)):
        zz = lax.rem(z - dz + 8, 8)
        for i, dx in enumerate(places):
            block = ((zz * 4 + lax.rem(x - dx + 4, 4)) * 2 + cc) * 2
            for b in range(2):
                target = pl.multiple_of(CHUNK + order_ref[block + b] * BLK, BLK)
                row = first_row + i * step + b * 64
                keys_values[pl.ds(target, BLK), :] = src[row : row + 64, :]

    for pack, dz in zip(packs, (0, 1, 7, 2, 6, 3, 5)):
        place(pack, 64, 192, dz, c)
    place(far_r, 64, 192, 4, c, (0, 1))
    place(far_l, 64, 192, 4, c, (2, 3))
    for i, dz in enumerate((0, 1, 7)):
        place(swap_a, i * 512, 128, dz, 1 - c)
    for i, dz in enumerate((2, 6, 3, 5)):
        place(swap_b, i * 512, 128, dz, 1 - c)
    place(swap_c, 0, 128, 4, 1 - c)

    for rb in range(ROW_BLOCKS):
        rows = slice((rb % 2) * 64, (rb % 2) * 64 + 64)
        both = (qt_keep[rb // 2, rows, :] + qt_received[rb // 2, rows, :]).astype(BF16)
        query_tangent[rb, 0:64, :] = both[:, 0:128]
        query_tangent[rb, 64:128, :] = both[:, 128:256]

    total = jnp.int32(0)
    for d in range(NDOC):
        total = total + lengths_ref[d]
        ends[d] = total
    packed_block = []
    extras = jnp.int32(0)
    sub = lax.broadcasted_iota(I32, (BLK, LANES), 0)
    lane = lax.broadcasted_iota(I32, (BLK, LANES), 1)
    for rb in range(ROW_BLOCKS):
        xx = lax.rem(x - rb // 2 + 4, 4)
        p = order_ref[((z * 4 + xx) * 2 + c) * 2 + rb % 2]
        packed_block.append(p)
        first = jnp.int32(0)
        start = jnp.zeros((BLK, LANES), I32)
        for d in range(NDOC):
            end = ends[d]
            first = jnp.where(end <= p * BLK, end, first)
            start = jnp.where(end <= p * BLK + sub, end, start)
        starts[rb] = start
        more = (p * BLK + BLK - first + CHUNK - 1) // CHUNK - 1

        def note(j, at, rb=rb, p=p):
            extra_block[at] = rb
            extra_row[at] = p * BLK + BLK - CHUNK * (j + 1)
            return at + 1

        extras = lax.fori_loop(0, more, note, extras)
    extra_block[extras] = ROW_BLOCKS
    extra_row[extras] = 0
    sums[ROW_BLOCKS] = jnp.zeros((4, BLK, LANES), F32)
    stats[ROW_BLOCKS] = jnp.zeros((4, BLK, LANES), F32)
    second[ROW_BLOCKS] = jnp.zeros((BLK, LANES), F32)
    starts[ROW_BLOCKS] = jnp.zeros((BLK, LANES), I32)

    def dot_t(a, b):
        return lax.dot_general(a, b, (((1,), (1,)), ((), ())), preferred_element_type=F32)

    def scored(rb, source, row, slot, last_pos):
        kv = keys_values[pl.ds(pl.multiple_of(row, BLK), CHUNK), :]
        st = dot_t(query_tangent[source], kv[:, 0:128])
        v = dot_t(upstream_ref[source], kv[:, 128:256])
        start = starts[rb]
        parts = [None] * 4
        for i in range(CHUNK // LANES):
            cut = slice(i * LANES, (i + 1) * LANES)
            key_pos = row - CHUNK + i * LANES + lane
            allowed = key_pos >= start
            if last_pos is not None:
                allowed = allowed & (key_pos <= last_pos)
            e = jnp.where(allowed, jnp.exp2(st[0:64, cut] * (SCALE * LOG2E)), 0.0)
            t_i, v_i = st[64:128, cut], v[:, cut]
            exp_buf[slot, :, cut] = e
            tan_buf[slot, :, cut] = t_i
            val_buf[slot, :, cut] = v_i
            ev = e * v_i
            for n, term in enumerate((e, ev, e * t_i, ev * t_i)):
                parts[n] = term if parts[n] is None else parts[n] + term
        return parts

    def weighted(rb, row, slot):
        value_mean, tangent_mean, drift, inverse = [stats[rb, n] for n in range(4)]
        pieces = []
        for i in range(CHUNK // LANES):
            cut = slice(i * LANES, (i + 1) * LANES)
            w = (exp_buf[slot, :, cut] * inverse) * (
                (tan_buf[slot, :, cut] - tangent_mean) * (val_buf[slot, :, cut] - value_mean)
                - drift
            )
            pieces.append(w.astype(BF16))
        keys = keys_values[pl.ds(pl.multiple_of(row, BLK), CHUNK), 0:128]
        return jnp.dot(jnp.concatenate(pieces, axis=1), keys, preferred_element_type=F32)

    for rb in range(ROW_BLOCKS):
        row = packed_block[rb] * BLK + BLK
        parts = scored(rb, rb, row, rb, packed_block[rb] * BLK + sub)
        for n in range(4):
            sums[rb, n] = parts[n]

    pairs = (extras + 1) // 2

    def extra_scores(i, carry):
        for item in (2 * i, 2 * i + 1):
            rb = extra_block[item]
            row = extra_row[item]
            parts = scored(rb, jnp.minimum(rb, ROW_BLOCKS - 1), row, ROW_BLOCKS + item, None)
            for n in range(4):
                sums[rb, n] += parts[n]
        return carry

    lax.fori_loop(0, pairs, extra_scores, 0)

    for rb in range(ROW_BLOCKS):
        weight_sum, value_sum, tangent_sum, joint_sum = [
            jnp.sum(sums[rb, n], axis=1, keepdims=True) for n in range(4)
        ]
        inverse = 1.0 / weight_sum
        value_mean = value_sum * inverse
        tangent_mean = tangent_sum * inverse
        drift = joint_sum * inverse - tangent_mean * value_mean
        for n, stat in enumerate((value_mean, tangent_mean, drift, inverse)):
            stats[rb, n] = jnp.broadcast_to(stat, (BLK, LANES))
    for rb in range(ROW_BLOCKS):
        second[rb] = weighted(rb, packed_block[rb] * BLK + BLK, rb)

    def extra_weights(i, carry):
        for item in (2 * i, 2 * i + 1):
            rb = extra_block[item]
            second[rb] += weighted(rb, extra_row[item], ROW_BLOCKS + item)
        return carry

    lax.fori_loop(0, pairs, extra_weights, 0)

    second_ref[...] = (
        second[0:ROW_BLOCKS].reshape(512, 128) * (SCALE * SCALE)
    ).astype(BF16)


def curvature_kernel(*refs):
    where_ref, hidden = refs[0], refs[1:6]
    second_own, second_other, out_ref, second_t, total = refs[6:]
    c, y = where_ref[2], where_ref[3]
    for dx in range(4):
        rows = slice(dx * 128, dx * 128 + 128)
        both = jnp.concatenate([second_own[rows, :], second_other[rows, :]], axis=0)
        second_t[dx] = both.astype(F32).T.astype(BF16)
    total[...] = jnp.zeros((4, 128, 512), F32)
    for r in range(4):
        for s in range(4):
            dx = jnp.where(c == 0, r, s)
            dy = jnp.where(c == 0, s, r)
            group = lax.rem(y - dy + 4, 4)
            total[group] += jnp.dot(
                second_t[dx], hidden_piece(hidden, r, s), preferred_element_type=F32
            )
    for g in range(4):
        out_ref[g * 512 : g * 512 + 512, :] = total[g].T.astype(BF16)


def gather_kernel(*refs):
    packs, (mine_ref, upstream_ref) = refs[:4], refs[4:]
    for dx, pack in enumerate(packs):
        mine_ref[dx * 192 : dx * 192 + 192, :] = pack[0:192, :]
        upstream_ref[2 * dx] = pack[192:256, 0:128]
        upstream_ref[2 * dx + 1] = pack[192:256, 128:256]


def keys_kernel(*refs):
    packs, out_ref = refs[:-1], refs[-1]
    at = 0
    for pack in packs:
        for dx in range(pack.shape[0] // 192):
            out_ref[at : at + 128, :] = pack[dx * 192 + 64 : dx * 192 + 192, :]
            at += 128


SMEM_SPEC = pl.BlockSpec(memory_space=pltpu.SMEM)
VMEM_SPEC = pl.BlockSpec(memory_space=pltpu.VMEM)


def call(kernel, scalars, arrays, out_shape, scratch, mebibytes, flops):
    return pl.pallas_call(
        kernel,
        out_shape=out_shape,
        in_specs=[SMEM_SPEC] * len(scalars) + [VMEM_SPEC] * len(arrays),
        out_specs=jax.tree.map(lambda _: VMEM_SPEC, out_shape),
        scratch_shapes=scratch,
        compiler_params=pltpu.CompilerParams(vmem_limit_bytes=mebibytes * 1024 * 1024),
        cost_estimate=pl.CostEstimate(flops=flops, bytes_accessed=8_000_000, transcendentals=0),
    )(*scalars, *arrays)


def prepare(where, arrays):
    any_spec = pl.BlockSpec(memory_space=pl.ANY)
    pack = jax.ShapeDtypeStruct((256, 256), BF16)
    half = jax.ShapeDtypeStruct((128, 512), BF16)
    return pl.pallas_call(
        prepare_kernel,
        out_shape=(pack,) * 4 + (half,) * 2,
        in_specs=[SMEM_SPEC] + [any_spec] * 6,
        out_specs=(VMEM_SPEC,) * 6,
        scratch_shapes=[pltpu.VMEM(a.shape, BF16) for a in arrays]
        + [pltpu.SemaphoreType.DMA((6,))],
        compiler_params=pltpu.CompilerParams(vmem_limit_bytes=60 * 1024 * 1024),
        cost_estimate=pl.CostEstimate(flops=1_000_000, bytes_accessed=600_000, transcendentals=0),
    )(where, *arrays)


def gather(packs):
    shapes = (
        jax.ShapeDtypeStruct((768, 256), BF16),
        jax.ShapeDtypeStruct((ROW_BLOCKS, BLK, HD), BF16),
    )
    return call(gather_kernel, (), packs, shapes, [], 2, 100_000)


def keys_of(packs):
    rows = sum(p.shape[0] // 192 * 128 for p in packs)
    return call(keys_kernel, (), packs, jax.ShapeDtypeStruct((rows, 256), BF16), [], 2, 100_000)


def project(where, arrays):
    shape = jax.ShapeDtypeStruct((4, 128, 256), F32)
    scratch = [pltpu.VMEM((8, 4, 64, 256), BF16), pltpu.VMEM((4, 256, 256), F32)]
    return call(project_kernel, (where,), arrays, (shape, shape), scratch, 6, 1_000_000_000)


def attend(scalars, arrays):
    scratch = [
        pltpu.VMEM((CHUNK + TOKENS, 256), BF16),
        pltpu.VMEM((ROW_BLOCKS, 128, 128), BF16),
        pltpu.VMEM((ROW_BLOCKS + 1, BLK, LANES), I32),
        pltpu.VMEM((ROW_BLOCKS + MOST_EXTRA + 1, BLK, CHUNK), F32),
        pltpu.VMEM((ROW_BLOCKS + MOST_EXTRA + 1, BLK, CHUNK), F32),
        pltpu.VMEM((ROW_BLOCKS + MOST_EXTRA + 1, BLK, CHUNK), F32),
        pltpu.VMEM((ROW_BLOCKS + 1, 4, BLK, LANES), F32),
        pltpu.VMEM((ROW_BLOCKS + 1, 4, BLK, LANES), F32),
        pltpu.VMEM((ROW_BLOCKS + 1, BLK, LANES), F32),
        pltpu.SMEM((NDOC,), I32),
        pltpu.SMEM((MOST_EXTRA + 1,), I32),
        pltpu.SMEM((MOST_EXTRA + 1,), I32),
    ]
    shape = jax.ShapeDtypeStruct((512, 128), BF16)
    return call(attend_kernel, scalars, arrays, shape, scratch, 26, 2_000_000_000)


def curvature(where, arrays):
    shape = jax.ShapeDtypeStruct((2048, 128), BF16)
    scratch = [pltpu.VMEM((4, 128, 256), BF16), pltpu.VMEM((4, 128, 512), F32)]
    return call(curvature_kernel, (where,), arrays, shape, scratch, 6, 600_000_000)


def shift(value, axis, size, step):
    return lax.ppermute(value, axis, [(i, (i + step) % size) for i in range(size)])


def swap(value):
    return shift(value, "c", 2, 1)


def shift_plane(value, step, first):
    pairs = []
    for i in range(4):
        for c in range(2):
            for j in range(4):
                along_y = (c == 0) == first
                ii, jj = (i, (j + step) % 4) if along_y else ((i + step) % 4, j)
                pairs.append(((i * 2 + c) * 4 + j, (ii * 2 + c) * 4 + jj))
    return lax.ppermute(value, ("x", "c", "kvh"), pairs)


def per_device(
    hidden, query_weight, probe_vector, key_rows, value_rows, upstream, lengths, block_order
):
    z = lax.axis_index("z")
    x = lax.axis_index("x")
    c = lax.axis_index("c")
    y = lax.axis_index("kvh")
    where = jnp.stack([z, x, c, y]).astype(I32)

    *packs, keep, send = prepare(
        where, (hidden, query_weight, probe_vector, key_rows, value_rows, upstream)
    )
    base = jnp.concatenate([keep, swap(send)], axis=0)
    *packs, base = lax.optimization_barrier((*packs, base))
    packs = [packs[0]] + [shift(packs[dx], "x", 4, dx) for dx in (1, 2, 3)]
    mine, upstream_rows = gather(packs)
    right_1, left_1 = shift(mine, "z", 8, 1), shift(mine, "z", 8, 7)

    stack = jnp.stack([base] + [shift_plane(base, s, True) for s in (1, 2, 3)])
    hid_right = shift_plane(stack, 1, False)
    hid_left = shift_plane(stack, 3, False)

    right_1, left_1, _ = lax.optimization_barrier((right_1, left_1, stack))
    right_2, left_2 = shift(right_1, "z", 8, 1), shift(left_1, "z", 8, 7)

    right_3, left_3 = shift(right_2, "z", 8, 1), shift(left_2, "z", 8, 7)
    swap_a = swap(keys_of((mine, right_1, left_1)))

    hid_far_a = shift_plane(hid_right[:2], 1, False)
    hid_far_b = shift_plane(hid_left[2:], 3, False)
    right_3, left_3, _ = lax.optimization_barrier((right_3, left_3, hid_right))
    far_r, far_l = shift(right_3[:384], "z", 8, 1), shift(left_3[384:], "z", 8, 7)
    swap_b = swap(keys_of((right_2, left_2, right_3, left_3)))
    pieces = (stack, hid_right, hid_left, hid_far_a, hid_far_b)

    ring = (mine, right_1, left_1, right_2, left_2, right_3, left_3)
    qt_keep, qt_send = project(where, (*pieces, *ring, far_r, far_l))
    qt_received = swap(qt_send)
    swap_c = swap(keys_of((far_r, far_l)))
    second_own = attend(
        (where, block_order, lengths),
        (
            qt_keep,
            qt_received,
            *ring,
            far_r,
            far_l,
            swap_a,
            swap_b,
            swap_c,
            upstream_rows,
        ),
    )
    second_other = swap(second_own)
    partial = curvature(where, (*pieces, second_own, second_other))
    shares = lax.all_to_all(partial, ("z", "x"), 0, 0, tiled=True)
    summed = jnp.sum(shares.reshape(8, 4, 64, 128).astype(F32), axis=0)
    return summed.transpose(1, 0, 2).reshape(64, 512)


def solution(mesh):
    fine = Mesh(mesh.devices.reshape(8, 4, 2, 4), ("z", "x", "c", "kvh"))
    ctx = ("z", "x", "c")
    split = P(ctx, "kvh")
    return jax.shard_map(
        per_device,
        mesh=fine,
        in_specs=(split,) * 6 + (P(), P()),
        out_specs=split,
        check_vma=False,
    )
```

```python
import math

import jax
import jax.numpy as jnp
from jax import lax
from jax.experimental import pallas as pl
from jax.experimental.pallas import tpu as pltpu
from jax.sharding import Mesh, PartitionSpec as P

HD = 128
BLK = 64
NDOC = 16
CHUNK = 512
LANES = 128
ROW_BLOCKS = 8
MOST_EXTRA = ROW_BLOCKS * 4
TOGETHER = 4
ORDER = 4
LENGTHS = ORDER + 128
SCALE = 1.0 / math.sqrt(HD)
LOG2E = 1.4426950408889634
TOKENS = 8192
BF16 = jnp.bfloat16
F32 = jnp.float32
I32 = jnp.int32


def prepare_kernel(
    where_ref,
    hidden_hbm,
    query_hbm,
    probe_hbm,
    key_hbm,
    value_hbm,
    upstream_hbm,
    pack0_ref,
    pack1_ref,
    pack2_ref,
    pack3_ref,
    keep_ref,
    send_ref,
    hidden_ref,
    query_ref,
    probe_ref,
    key_ref,
    value_ref,
    upstream_ref,
    sems,
):
    x, c = where_ref[1], where_ref[2]
    copies = [
        pltpu.make_async_copy(src, dst, sems.at[i])
        for i, (src, dst) in enumerate(
            (
                (query_hbm, query_ref),
                (probe_hbm, probe_ref),
                (key_hbm, key_ref),
                (value_hbm, value_ref),
                (upstream_hbm, upstream_ref),
                (hidden_hbm, hidden_ref),
            )
        )
    ]
    for copy in copies:
        copy.start()
    for copy in copies[:5]:
        copy.wait()
    for dx, pack in enumerate((pack0_ref, pack1_ref, pack2_ref, pack3_ref)):
        columns = pl.ds(pl.multiple_of(lax.rem(x + dx, 4) * HD, HD), HD)
        pack[0:64, 0:128] = query_ref[:, columns]
        pack[0:64, 128:256] = probe_ref[:, columns]
        pack[64:192, 0:128] = key_ref[...]
        pack[64:192, 128:256] = value_ref[...]
        pack[192:256, 0:128] = upstream_ref[0:64, columns]
        pack[192:256, 128:256] = upstream_ref[64:128, columns]
    copies[5].wait()
    low = lax.broadcasted_iota(I32, (128, 128), 1) < 64
    for k in range(4):
        a = hidden_ref[:, 256 * k : 256 * k + 128].astype(F32)
        b = hidden_ref[:, 256 * k + 128 : 256 * k + 256].astype(F32)
        first = jnp.where(low, a, pltpu.roll(b, 64, 1))
        second = jnp.where(low, pltpu.roll(a, 64, 1), b)
        cut = slice(128 * k, 128 * k + 128)
        keep_ref[:, cut] = jnp.where(c == 0, first, second).astype(BF16)
        send_ref[:, cut] = jnp.where(c == 0, second, first).astype(BF16)


def hidden_piece(refs, r, s):
    return refs[r][s]


def project_kernel(*refs):
    where_ref, hidden = refs[0], refs[1:5]
    packs, far_r, far_l = refs[5:12], refs[12], refs[13]
    keep_ref, send_ref, weights, total = refs[14:]
    z, x, c, y = where_ref[0], where_ref[1], where_ref[2], where_ref[3]

    def place(pack, dz, places=(0, 1, 2, 3)):
        for i, dx in enumerate(places):
            weights[lax.rem(z - dz + 8, 8), lax.rem(x - dx + 4, 4)] = pack[
                i * 192 : i * 192 + 64, :
            ]

    for pack, dz in zip(packs, (0, 1, 7, 2, 6, 3, 5)):
        place(pack, dz)
    place(far_r, 4, (0, 1))
    place(far_l, 4, (2, 3))

    total[...] = jnp.zeros((4, 256, 256), F32)
    for r in range(4):
        for s in range(4):
            dx = jnp.where(c == 0, r, s)
            dy = jnp.where(c == 0, s, r)
            group = lax.rem(y - dy + 4, 4)
            w = weights[pl.ds(group * 2, 2)].reshape(512, 256)
            total[dx] += jnp.dot(hidden_piece(hidden, r, s), w, preferred_element_type=F32)
    keep_ref[...] = total[:, 0:128, :]
    send_ref[...] = total[:, 128:256, :]


def attend_kernel(*refs):
    where_ref, qt_keep, qt_received = refs[:3]
    packs, far_r, far_l = refs[3:10], refs[10], refs[11]
    swap_a, swap_b, swap_c = refs[12:15]
    upstream_ref, second_ref = refs[15:17]
    (
        keys_values,
        query_tangent,
        starts,
        scores,
        sums,
        stats,
        second,
        ends,
        extra_block,
        extra_row,
    ) = refs[17:]
    z, x, c = where_ref[0], where_ref[1], where_ref[2]

    keys_values[0:CHUNK, :] = jnp.zeros((CHUNK, 256), BF16)

    def place(src, first_row, step, dz, cc, places=(0, 1, 2, 3)):
        zz = lax.rem(z - dz + 8, 8)
        for i, dx in enumerate(places):
            block = ((zz * 4 + lax.rem(x - dx + 4, 4)) * 2 + cc) * 2
            for b in range(2):
                target = pl.multiple_of(CHUNK + where_ref[ORDER + block + b] * BLK, BLK)
                row = first_row + i * step + b * 64
                keys_values[pl.ds(target, BLK), :] = src[row : row + 64, :]

    for pack, dz in zip(packs, (0, 1, 7, 2, 6, 3, 5)):
        place(pack, 64, 192, dz, c)
    place(far_r, 64, 192, 4, c, (0, 1))
    place(far_l, 64, 192, 4, c, (2, 3))
    for i, dz in enumerate((0, 1, 7)):
        place(swap_a, i * 512, 128, dz, 1 - c)
    for i, dz in enumerate((2, 6, 3, 5)):
        place(swap_b, i * 512, 128, dz, 1 - c)
    place(swap_c, 0, 128, 4, 1 - c)

    for rb in range(ROW_BLOCKS):
        rows = slice((rb % 2) * 64, (rb % 2) * 64 + 64)
        both = (qt_keep[rb // 2, rows, :] + qt_received[rb // 2, rows, :]).astype(BF16)
        query_tangent[rb, 0:64, :] = both[:, 0:128]
        query_tangent[rb, 64:128, :] = both[:, 128:256]

    total = jnp.int32(0)
    for d in range(NDOC):
        total = total + where_ref[LENGTHS + d]
        ends[d] = total
    packed_block = []
    extras = jnp.int32(0)
    sub = lax.broadcasted_iota(I32, (BLK, LANES), 0)
    lane = lax.broadcasted_iota(I32, (BLK, LANES), 1)
    for rb in range(ROW_BLOCKS):
        xx = lax.rem(x - rb // 2 + 4, 4)
        p = where_ref[ORDER + ((z * 4 + xx) * 2 + c) * 2 + rb % 2]
        packed_block.append(p)
        first = jnp.int32(0)
        start = jnp.zeros((BLK, LANES), I32)
        for d in range(NDOC):
            end = ends[d]
            first = jnp.where(end <= p * BLK, end, first)
            start = jnp.where(end <= p * BLK + sub, end, start)
        starts[rb] = start
        more = (p * BLK + BLK - first + CHUNK - 1) // CHUNK - 1

        def note(j, at, rb=rb, p=p):
            extra_block[at] = rb
            extra_row[at] = p * BLK + BLK - CHUNK * (j + 1)
            return at + 1

        extras = lax.fori_loop(0, more, note, extras)
    for n in range(TOGETHER - 1):
        extra_block[extras + n] = ROW_BLOCKS
        extra_row[extras + n] = 0
    sums[ROW_BLOCKS] = jnp.zeros((4, BLK, LANES), F32)
    stats[ROW_BLOCKS] = jnp.zeros((4, BLK, LANES), F32)
    second[ROW_BLOCKS] = jnp.zeros((BLK, LANES), F32)
    starts[ROW_BLOCKS] = jnp.zeros((BLK, LANES), I32)

    def dot_t(a, b):
        return lax.dot_general(a, b, (((1,), (1,)), ((), ())), preferred_element_type=F32)

    def scored(rb, source, row, last_pos):
        kv = keys_values[pl.ds(pl.multiple_of(row, BLK), CHUNK), :]
        st = dot_t(query_tangent[source], kv[:, 0:128])
        v = dot_t(upstream_ref[source], kv[:, 128:256])
        start = starts[rb]
        parts = []
        for i in range(CHUNK // LANES):
            cut = slice(i * LANES, (i + 1) * LANES)
            key_pos = row - CHUNK + i * LANES + lane
            allowed = key_pos >= start
            if last_pos is not None:
                allowed = allowed & (key_pos <= last_pos)
            e = jnp.where(allowed, jnp.exp2(st[0:64, cut] * (SCALE * LOG2E)), 0.0)
            parts.append((e, st[64:128, cut], v[:, cut]))
        return parts

    def row_sums(parts):
        out = [None] * 4
        for e, t, v in parts:
            ev = e * v
            for n, term in enumerate((e, ev, e * t, ev * t)):
                out[n] = term if out[n] is None else out[n] + term
        return out

    def keep_scores(slot, parts):
        for i, part in enumerate(parts):
            for n in range(3):
                scores[slot, n, :, i * LANES : (i + 1) * LANES] = part[n]

    def kept_scores(slot):
        cuts = [slice(i * LANES, (i + 1) * LANES) for i in range(CHUNK // LANES)]
        return [[scores[slot, n, :, cut] for n in range(3)] for cut in cuts]

    def weighted(rb, row, parts):
        value_mean, tangent_mean, drift, inverse = [stats[rb, n] for n in range(4)]
        pieces = []
        for e, t, v in parts:
            w = (e * inverse) * ((t - tangent_mean) * (v - value_mean) - drift)
            pieces.append(w.astype(BF16))
        keys = keys_values[pl.ds(pl.multiple_of(row, BLK), CHUNK), 0:128]
        return jnp.dot(jnp.concatenate(pieces, axis=1), keys, preferred_element_type=F32)

    for rb in range(ROW_BLOCKS):
        p = packed_block[rb]
        parts = scored(rb, rb, p * BLK + BLK, p * BLK + sub)
        keep_scores(rb, parts)
        for n, total in enumerate(row_sums(parts)):
            sums[rb, n] = total

    rounds = (extras + TOGETHER - 1) // TOGETHER

    def extra_scores(i, carry):
        for item in [TOGETHER * i + n for n in range(TOGETHER)]:
            rb = extra_block[item]
            parts = scored(rb, jnp.minimum(rb, ROW_BLOCKS - 1), extra_row[item], None)
            keep_scores(ROW_BLOCKS + item, parts)
            for n, total in enumerate(row_sums(parts)):
                sums[rb, n] += total
        return carry

    lax.fori_loop(0, rounds, extra_scores, 0)

    for rb in range(ROW_BLOCKS):
        weight_sum, value_sum, tangent_sum, joint_sum = [
            jnp.sum(sums[rb, n], axis=1, keepdims=True) for n in range(4)
        ]
        inverse = 1.0 / weight_sum
        value_mean = value_sum * inverse
        tangent_mean = tangent_sum * inverse
        drift = joint_sum * inverse - tangent_mean * value_mean
        for n, stat in enumerate((value_mean, tangent_mean, drift, inverse)):
            stats[rb, n] = jnp.broadcast_to(stat, (BLK, LANES))
    for rb in range(ROW_BLOCKS):
        second[rb] = weighted(rb, packed_block[rb] * BLK + BLK, kept_scores(rb))

    def extra_weights(i, carry):
        for item in [TOGETHER * i + n for n in range(TOGETHER)]:
            rb = extra_block[item]
            row = extra_row[item]
            second[rb] += weighted(rb, row, kept_scores(ROW_BLOCKS + item))
        return carry

    lax.fori_loop(0, rounds, extra_weights, 0)

    second_ref[...] = (
        second[0:ROW_BLOCKS].reshape(512, 128) * (SCALE * SCALE)
    ).astype(BF16)


def curvature_kernel(*refs):
    where_ref, hidden = refs[0], refs[1:5]
    second_own, second_other, out_ref, second_t, total = refs[5:]
    c, y = where_ref[2], where_ref[3]
    for dx in range(4):
        rows = slice(dx * 128, dx * 128 + 128)
        both = jnp.concatenate([second_own[rows, :], second_other[rows, :]], axis=0)
        second_t[dx] = both.astype(F32).T.astype(BF16)
    total[...] = jnp.zeros((4, 128, 512), F32)
    for r in range(4):
        for s in range(4):
            dx = jnp.where(c == 0, r, s)
            dy = jnp.where(c == 0, s, r)
            group = lax.rem(y - dy + 4, 4)
            total[group] += jnp.dot(
                second_t[dx], hidden_piece(hidden, r, s), preferred_element_type=F32
            )
    for g in range(4):
        out_ref[g * 512 : g * 512 + 512, :] = total[g].T.astype(BF16)


def gather_kernel(*refs):
    packs, (mine_ref, upstream_ref) = refs[1:5], refs[5:]
    for dx, pack in enumerate(packs):
        mine_ref[dx * 192 : dx * 192 + 192, :] = pack[0:192, :]
        upstream_ref[2 * dx] = pack[192:256, 0:128]
        upstream_ref[2 * dx + 1] = pack[192:256, 128:256]


def keys_kernel(*refs):
    packs, out_ref = refs[:-1], refs[-1]
    at = 0
    for pack in packs:
        for dx in range(pack.shape[0] // 192):
            out_ref[at : at + 128, :] = pack[dx * 192 + 64 : dx * 192 + 192, :]
            at += 128


SMEM_SPEC = pl.BlockSpec(memory_space=pltpu.SMEM)
VMEM_SPEC = pl.BlockSpec(memory_space=pltpu.VMEM)


def call(kernel, scalars, arrays, out_shape, scratch, mebibytes, flops):
    return pl.pallas_call(
        kernel,
        out_shape=out_shape,
        in_specs=[SMEM_SPEC] * len(scalars) + [VMEM_SPEC] * len(arrays),
        out_specs=jax.tree.map(lambda _: VMEM_SPEC, out_shape),
        scratch_shapes=scratch,
        compiler_params=pltpu.CompilerParams(vmem_limit_bytes=mebibytes * 1024 * 1024),
        cost_estimate=pl.CostEstimate(flops=flops, bytes_accessed=8_000_000, transcendentals=0),
    )(*scalars, *arrays)


def prepare(where, arrays):
    any_spec = pl.BlockSpec(memory_space=pl.ANY)
    pack = jax.ShapeDtypeStruct((256, 256), BF16)
    half = jax.ShapeDtypeStruct((128, 512), BF16)
    return pl.pallas_call(
        prepare_kernel,
        out_shape=(pack,) * 4 + (half,) * 2,
        in_specs=[SMEM_SPEC] + [any_spec] * 6,
        out_specs=(VMEM_SPEC,) * 6,
        scratch_shapes=[pltpu.VMEM(a.shape, BF16) for a in arrays]
        + [pltpu.SemaphoreType.DMA((6,))],
        compiler_params=pltpu.CompilerParams(vmem_limit_bytes=2 * 1024 * 1024),
        cost_estimate=pl.CostEstimate(flops=1_000_000, bytes_accessed=600_000, transcendentals=0),
    )(where, *arrays)


def gather(scalars, packs):
    shapes = (
        jax.ShapeDtypeStruct((768, 256), BF16),
        jax.ShapeDtypeStruct((ROW_BLOCKS, BLK, HD), BF16),
    )
    return call(gather_kernel, (scalars,), packs, shapes, [], 2, 100_000)


def keys_of(packs, flops=100_000):
    rows = sum(p.shape[0] // 192 * 128 for p in packs)
    return call(keys_kernel, (), packs, jax.ShapeDtypeStruct((rows, 256), BF16), [], 2, flops)


def project(where, arrays):
    shape = jax.ShapeDtypeStruct((4, 128, 256), F32)
    scratch = [pltpu.VMEM((8, 4, 64, 256), BF16), pltpu.VMEM((4, 256, 256), F32)]
    return call(project_kernel, (where,), arrays, (shape, shape), scratch, 6, 1_000_000_000)


def attend(scalars, arrays):
    scratch = [
        pltpu.VMEM((CHUNK + TOKENS, 256), BF16),
        pltpu.VMEM((ROW_BLOCKS, 128, 128), BF16),
        pltpu.VMEM((ROW_BLOCKS + 1, BLK, LANES), I32),
        pltpu.VMEM((ROW_BLOCKS + MOST_EXTRA, 3, BLK, CHUNK), F32),
        pltpu.VMEM((ROW_BLOCKS + 1, 4, BLK, LANES), F32),
        pltpu.VMEM((ROW_BLOCKS + 1, 4, BLK, LANES), F32),
        pltpu.VMEM((ROW_BLOCKS + 1, BLK, LANES), F32),
        pltpu.SMEM((NDOC,), I32),
        pltpu.SMEM((MOST_EXTRA + TOGETHER,), I32),
        pltpu.SMEM((MOST_EXTRA + TOGETHER,), I32),
    ]
    shape = jax.ShapeDtypeStruct((512, 128), BF16)
    return call(attend_kernel, scalars, arrays, shape, scratch, 27, 2_000_000_000)


def curvature(where, arrays):
    shape = jax.ShapeDtypeStruct((2048, 128), BF16)
    scratch = [pltpu.VMEM((4, 128, 256), BF16), pltpu.VMEM((4, 128, 512), F32)]
    return call(curvature_kernel, (where,), arrays, shape, scratch, 6, 600_000_000)


def shift(value, axis, size, step):
    return lax.ppermute(value, axis, [(i, (i + step) % size) for i in range(size)])


def swap(value):
    return shift(value, "c", 2, 1)


def shift_plane(value, step, first):
    pairs = []
    for i in range(4):
        for c in range(2):
            for j in range(4):
                along_y = (c == 0) == first
                ii, jj = (i, (j + step) % 4) if along_y else ((i + step) % 4, j)
                pairs.append(((i * 2 + c) * 4 + j, (ii * 2 + c) * 4 + jj))
    return lax.ppermute(value, ("x", "c", "kvh"), pairs)


def per_device(
    hidden, query_weight, probe_vector, key_rows, value_rows, upstream, lengths, block_order
):
    z = lax.axis_index("z")
    x = lax.axis_index("x")
    c = lax.axis_index("c")
    y = lax.axis_index("kvh")
    where = jnp.stack([z, x, c, y]).astype(I32)
    scalars = jnp.concatenate([where, block_order, lengths])

    *packs, keep, send = prepare(
        where,
        tuple(
            pltpu.with_memory_space_constraint(a, pltpu.HBM)
            for a in (hidden, query_weight, probe_vector, key_rows, value_rows, upstream)
        ),
    )
    base = jnp.concatenate([keep, swap(send)], axis=0)
    packs = [packs[0]] + [shift(packs[dx], "x", 4, dx) for dx in (1, 2, 3)]
    base, *packs = lax.optimization_barrier((base, *packs))
    mine, upstream_rows = gather(scalars, packs)
    right_1, left_1 = shift(mine, "z", 8, 1), shift(mine, "z", 8, 7)

    stack = jnp.stack([base] + [shift_plane(base, s, True) for s in (1, 2, 3)])
    hid_right, hid_far, hid_left = [shift_plane(stack, n, False) for n in (1, 2, 3)]
    right_2, left_2 = shift(right_1, "z", 8, 1), shift(left_1, "z", 8, 7)

    right_3, left_3 = shift(right_2, "z", 8, 1), shift(left_2, "z", 8, 7)
    swap_a = swap(keys_of((mine, right_1, left_1)))

    far_r, far_l = shift(right_3[:384], "z", 8, 1), shift(left_3[384:], "z", 8, 7)
    *late, hid_right = lax.optimization_barrier((right_2, left_2, right_3, left_3, hid_right))
    swap_b = swap(keys_of(late))
    pieces = (stack, hid_right, hid_far, hid_left)

    ring = (mine, right_1, left_1, right_2, left_2, right_3, left_3)
    qt_keep, qt_send = project(where, (*pieces, *ring, far_r, far_l))
    qt_received = swap(qt_send)
    swap_c = swap(keys_of((far_r, far_l), 20000000000))
    second_own = attend(
        (scalars,),
        (
            qt_keep,
            qt_received,
            *ring,
            far_r,
            far_l,
            swap_a,
            swap_b,
            swap_c,
            upstream_rows,
        ),
    )
    second_other = swap(second_own)
    partial = curvature(where, (*pieces, second_own, second_other))
    shares = lax.all_to_all(partial, ("z", "x"), 0, 0, tiled=True)
    summed = jnp.sum(shares.reshape(8, 4, 64, 128).astype(F32), axis=0)
    return summed.transpose(1, 0, 2).reshape(64, 512)


def solution(mesh):
    fine = Mesh(mesh.devices.reshape(8, 4, 2, 4), ("z", "x", "c", "kvh"))
    ctx = ("z", "x", "c")
    split = P(ctx, "kvh")
    return jax.shard_map(
        per_device,
        mesh=fine,
        in_specs=(split,) * 6 + (P(), P()),
        out_specs=split,
        check_vma=False,
    )
```

```python
import math

import jax
import jax.numpy as jnp
from jax import lax
from jax.experimental import pallas as pl
from jax.experimental.pallas import tpu as pltpu
from jax.sharding import Mesh, PartitionSpec as P

HD = 128
BLK = 64
NDOC = 16
CHUNK = 512
LANES = 128
ROW_BLOCKS = 8
MOST_EXTRA = ROW_BLOCKS * 4
TOGETHER = 4
ORDER = 4
LENGTHS = ORDER + 128
SCALE = 1.0 / math.sqrt(HD)
LOG2E = 1.4426950408889634
TOKENS = 8192
BF16 = jnp.bfloat16
F32 = jnp.float32
I32 = jnp.int32


def prepare_kernel(
    where_ref,
    hidden_hbm,
    query_hbm,
    probe_hbm,
    key_hbm,
    value_hbm,
    upstream_hbm,
    pack0_ref,
    pack1_ref,
    pack2_ref,
    pack3_ref,
    keep_ref,
    send_ref,
    hidden_ref,
    query_ref,
    probe_ref,
    key_ref,
    value_ref,
    upstream_ref,
    sems,
):
    x, c = where_ref[1], where_ref[2]
    copies = [
        pltpu.make_async_copy(src, dst, sems.at[i])
        for i, (src, dst) in enumerate(
            (
                (query_hbm, query_ref),
                (probe_hbm, probe_ref),
                (key_hbm, key_ref),
                (value_hbm, value_ref),
                (upstream_hbm, upstream_ref),
                (hidden_hbm, hidden_ref),
            )
        )
    ]
    for copy in copies:
        copy.start()
    for copy in copies[:5]:
        copy.wait()
    for dx, pack in enumerate((pack0_ref, pack1_ref, pack2_ref, pack3_ref)):
        columns = pl.ds(pl.multiple_of(lax.rem(x + dx, 4) * HD, HD), HD)
        pack[0:64, 0:128] = query_ref[:, columns]
        pack[0:64, 128:256] = probe_ref[:, columns]
        pack[64:192, 0:128] = key_ref[...]
        pack[64:192, 128:256] = value_ref[...]
        pack[192:256, 0:128] = upstream_ref[0:64, columns]
        pack[192:256, 128:256] = upstream_ref[64:128, columns]
    copies[5].wait()
    low = lax.broadcasted_iota(I32, (128, 128), 1) < 64
    for k in range(4):
        a = hidden_ref[:, 256 * k : 256 * k + 128].astype(F32)
        b = hidden_ref[:, 256 * k + 128 : 256 * k + 256].astype(F32)
        first = jnp.where(low, a, pltpu.roll(b, 64, 1))
        second = jnp.where(low, pltpu.roll(a, 64, 1), b)
        cut = slice(128 * k, 128 * k + 128)
        keep_ref[:, cut] = jnp.where(c == 0, first, second).astype(BF16)
        send_ref[:, cut] = jnp.where(c == 0, second, first).astype(BF16)


PLACE = (0, 2, 3, 1)


def hidden_piece(refs, r, s):
    return refs[PLACE[r]][PLACE[s]]


def project_kernel(*refs):
    where_ref, hidden = refs[0], refs[1:5]
    packs, far_r, far_l = refs[5:12], refs[12], refs[13]
    keep_ref, send_ref, weights, total = refs[14:]
    z, x, c, y = where_ref[0], where_ref[1], where_ref[2], where_ref[3]

    def place(pack, dz, places=(0, 1, 2, 3)):
        for i, dx in enumerate(places):
            weights[lax.rem(z - dz + 8, 8), lax.rem(x - dx + 4, 4)] = pack[
                i * 192 : i * 192 + 64, :
            ]

    for pack, dz in zip(packs, (0, 1, 7, 2, 6, 3, 5)):
        place(pack, dz)
    place(far_r, 4, (0, 1))
    place(far_l, 4, (2, 3))

    total[...] = jnp.zeros((4, 256, 256), F32)
    for r in range(4):
        for s in range(4):
            dx = jnp.where(c == 0, r, s)
            dy = jnp.where(c == 0, s, r)
            group = lax.rem(y - dy + 4, 4)
            w = weights[pl.ds(group * 2, 2)].reshape(512, 256)
            total[dx] += jnp.dot(hidden_piece(hidden, r, s), w, preferred_element_type=F32)
    keep_ref[...] = total[:, 0:128, :]
    send_ref[...] = total[:, 128:256, :]


def attend_kernel(*refs):
    where_ref, qt_keep, qt_received = refs[:3]
    packs, far_r, far_l = refs[3:10], refs[10], refs[11]
    swap_a, swap_b, swap_c = refs[12:15]
    upstream_ref, second_ref = refs[15:17]
    (
        keys_values,
        query_tangent,
        starts,
        scores,
        sums,
        stats,
        second,
        ends,
        extra_block,
        extra_row,
    ) = refs[17:]
    z, x, c = where_ref[0], where_ref[1], where_ref[2]

    keys_values[0:CHUNK, :] = jnp.zeros((CHUNK, 256), BF16)

    def place(src, first_row, step, dz, cc, places=(0, 1, 2, 3)):
        zz = lax.rem(z - dz + 8, 8)
        for i, dx in enumerate(places):
            block = ((zz * 4 + lax.rem(x - dx + 4, 4)) * 2 + cc) * 2
            for b in range(2):
                target = pl.multiple_of(CHUNK + where_ref[ORDER + block + b] * BLK, BLK)
                row = first_row + i * step + b * 64
                keys_values[pl.ds(target, BLK), :] = src[row : row + 64, :]

    for pack, dz in zip(packs, (0, 1, 7, 2, 6, 3, 5)):
        place(pack, 64, 192, dz, c)
    place(far_r, 64, 192, 4, c, (0, 1))
    place(far_l, 64, 192, 4, c, (2, 3))
    for i, dz in enumerate((0, 1, 7)):
        place(swap_a, i * 512, 128, dz, 1 - c)
    for i, dz in enumerate((2, 6, 3, 5)):
        place(swap_b, i * 512, 128, dz, 1 - c)
    place(swap_c, 0, 128, 4, 1 - c)

    for rb in range(ROW_BLOCKS):
        rows = slice((rb % 2) * 64, (rb % 2) * 64 + 64)
        both = (qt_keep[rb // 2, rows, :] + qt_received[rb // 2, rows, :]).astype(BF16)
        query_tangent[rb, 0:64, :] = both[:, 0:128]
        query_tangent[rb, 64:128, :] = both[:, 128:256]

    total = jnp.int32(0)
    for d in range(NDOC):
        total = total + where_ref[LENGTHS + d]
        ends[d] = total
    packed_block = []
    extras = jnp.int32(0)
    sub = lax.broadcasted_iota(I32, (BLK, LANES), 0)
    lane = lax.broadcasted_iota(I32, (BLK, LANES), 1)
    for rb in range(ROW_BLOCKS):
        xx = lax.rem(x - rb // 2 + 4, 4)
        p = where_ref[ORDER + ((z * 4 + xx) * 2 + c) * 2 + rb % 2]
        packed_block.append(p)
        first = jnp.int32(0)
        start = jnp.zeros((BLK, LANES), I32)
        for d in range(NDOC):
            end = ends[d]
            first = jnp.where(end <= p * BLK, end, first)
            start = jnp.where(end <= p * BLK + sub, end, start)
        starts[rb] = start
        more = (p * BLK + BLK - first + CHUNK - 1) // CHUNK - 1

        def note(j, at, rb=rb, p=p):
            extra_block[at] = rb
            extra_row[at] = p * BLK + BLK - CHUNK * (j + 1)
            return at + 1

        extras = lax.fori_loop(0, more, note, extras)
    for n in range(TOGETHER - 1):
        extra_block[extras + n] = ROW_BLOCKS
        extra_row[extras + n] = 0
    sums[ROW_BLOCKS] = jnp.zeros((4, BLK, LANES), F32)
    stats[ROW_BLOCKS] = jnp.zeros((4, BLK, LANES), F32)
    second[ROW_BLOCKS] = jnp.zeros((BLK, LANES), F32)
    starts[ROW_BLOCKS] = jnp.zeros((BLK, LANES), I32)

    def dot_t(a, b):
        return lax.dot_general(a, b, (((1,), (1,)), ((), ())), preferred_element_type=F32)

    def scored(rb, source, row, last_pos):
        kv = keys_values[pl.ds(pl.multiple_of(row, BLK), CHUNK), :]
        st = dot_t(query_tangent[source], kv[:, 0:128])
        v = dot_t(upstream_ref[source], kv[:, 128:256])
        start = starts[rb]
        parts = []
        for i in range(CHUNK // LANES):
            cut = slice(i * LANES, (i + 1) * LANES)
            key_pos = row - CHUNK + i * LANES + lane
            allowed = key_pos >= start
            if last_pos is not None:
                allowed = allowed & (key_pos <= last_pos)
            e = jnp.where(allowed, jnp.exp2(st[0:64, cut] * (SCALE * LOG2E)), 0.0)
            parts.append((e, st[64:128, cut], v[:, cut]))
        return parts

    def row_sums(parts):
        out = [None] * 4
        for e, t, v in parts:
            ev = e * v
            for n, term in enumerate((e, ev, e * t, ev * t)):
                out[n] = term if out[n] is None else out[n] + term
        return out

    def keep_scores(slot, parts):
        for i, part in enumerate(parts):
            for n in range(3):
                scores[slot, n, :, i * LANES : (i + 1) * LANES] = part[n]

    def kept_scores(slot):
        cuts = [slice(i * LANES, (i + 1) * LANES) for i in range(CHUNK // LANES)]
        return [[scores[slot, n, :, cut] for n in range(3)] for cut in cuts]

    def weighted(rb, row, parts):
        value_mean, tangent_mean, drift, inverse = [stats[rb, n] for n in range(4)]
        pieces = []
        for e, t, v in parts:
            w = (e * inverse) * ((t - tangent_mean) * (v - value_mean) - drift)
            pieces.append(w.astype(BF16))
        keys = keys_values[pl.ds(pl.multiple_of(row, BLK), CHUNK), 0:128]
        return jnp.dot(jnp.concatenate(pieces, axis=1), keys, preferred_element_type=F32)

    for rb in range(ROW_BLOCKS):
        p = packed_block[rb]
        parts = scored(rb, rb, p * BLK + BLK, p * BLK + sub)
        keep_scores(rb, parts)
        for n, total in enumerate(row_sums(parts)):
            sums[rb, n] = total

    rounds = (extras + TOGETHER - 1) // TOGETHER

    def extra_scores(i, carry):
        for item in [TOGETHER * i + n for n in range(TOGETHER)]:
            rb = extra_block[item]
            parts = scored(rb, jnp.minimum(rb, ROW_BLOCKS - 1), extra_row[item], None)
            keep_scores(ROW_BLOCKS + item, parts)
            for n, total in enumerate(row_sums(parts)):
                sums[rb, n] += total
        return carry

    lax.fori_loop(0, rounds, extra_scores, 0)

    for rb in range(ROW_BLOCKS):
        weight_sum, value_sum, tangent_sum, joint_sum = [
            jnp.sum(sums[rb, n], axis=1, keepdims=True) for n in range(4)
        ]
        inverse = 1.0 / weight_sum
        value_mean = value_sum * inverse
        tangent_mean = tangent_sum * inverse
        drift = joint_sum * inverse - tangent_mean * value_mean
        for n, stat in enumerate((value_mean, tangent_mean, drift, inverse)):
            stats[rb, n] = jnp.broadcast_to(stat, (BLK, LANES))
    for rb in range(ROW_BLOCKS):
        second[rb] = weighted(rb, packed_block[rb] * BLK + BLK, kept_scores(rb))

    def extra_weights(i, carry):
        for item in [TOGETHER * i + n for n in range(TOGETHER)]:
            rb = extra_block[item]
            row = extra_row[item]
            second[rb] += weighted(rb, row, kept_scores(ROW_BLOCKS + item))
        return carry

    lax.fori_loop(0, rounds, extra_weights, 0)

    second_ref[...] = (
        second[0:ROW_BLOCKS].reshape(512, 128) * (SCALE * SCALE)
    ).astype(BF16)


def curvature_kernel(*refs):
    where_ref, hidden = refs[0], refs[1:5]
    second_own, second_other, out_ref, second_t, total = refs[5:]
    c, y = where_ref[2], where_ref[3]
    for dx in range(4):
        rows = slice(dx * 128, dx * 128 + 128)
        both = jnp.concatenate([second_own[rows, :], second_other[rows, :]], axis=0)
        second_t[dx] = both.astype(F32).T.astype(BF16)
    total[...] = jnp.zeros((4, 128, 512), F32)
    for r in range(4):
        for s in range(4):
            dx = jnp.where(c == 0, r, s)
            dy = jnp.where(c == 0, s, r)
            group = lax.rem(y - dy + 4, 4)
            total[group] += jnp.dot(
                second_t[dx], hidden_piece(hidden, r, s), preferred_element_type=F32
            )
    for g in range(4):
        out_ref[g * 512 : g * 512 + 512, :] = total[g].T.astype(BF16)


def gather_kernel(*refs):
    packs, (mine_ref, upstream_ref) = refs[1:5], refs[5:]
    for dx, pack in enumerate(packs):
        mine_ref[dx * 192 : dx * 192 + 192, :] = pack[0:192, :]
        upstream_ref[2 * dx] = pack[192:256, 0:128]
        upstream_ref[2 * dx + 1] = pack[192:256, 128:256]


def keys_kernel(*refs):
    packs, out_ref = refs[:-1], refs[-1]
    at = 0
    for pack in packs:
        for dx in range(pack.shape[0] // 192):
            out_ref[at : at + 128, :] = pack[dx * 192 + 64 : dx * 192 + 192, :]
            at += 128


SMEM_SPEC = pl.BlockSpec(memory_space=pltpu.SMEM)
VMEM_SPEC = pl.BlockSpec(memory_space=pltpu.VMEM)


def call(kernel, scalars, arrays, out_shape, scratch, mebibytes, flops):
    return pl.pallas_call(
        kernel,
        out_shape=out_shape,
        in_specs=[SMEM_SPEC] * len(scalars) + [VMEM_SPEC] * len(arrays),
        out_specs=jax.tree.map(lambda _: VMEM_SPEC, out_shape),
        scratch_shapes=scratch,
        compiler_params=pltpu.CompilerParams(vmem_limit_bytes=mebibytes * 1024 * 1024),
        cost_estimate=pl.CostEstimate(flops=flops, bytes_accessed=8_000_000, transcendentals=0),
    )(*scalars, *arrays)


def prepare(where, arrays):
    any_spec = pl.BlockSpec(memory_space=pl.ANY)
    pack = jax.ShapeDtypeStruct((256, 256), BF16)
    half = jax.ShapeDtypeStruct((128, 512), BF16)
    return pl.pallas_call(
        prepare_kernel,
        out_shape=(pack,) * 4 + (half,) * 2,
        in_specs=[SMEM_SPEC] + [any_spec] * 6,
        out_specs=(VMEM_SPEC,) * 6,
        scratch_shapes=[pltpu.VMEM(a.shape, BF16) for a in arrays]
        + [pltpu.SemaphoreType.DMA((6,))],
        compiler_params=pltpu.CompilerParams(vmem_limit_bytes=2 * 1024 * 1024),
        cost_estimate=pl.CostEstimate(flops=1_000_000, bytes_accessed=600_000, transcendentals=0),
    )(where, *arrays)


def gather(scalars, packs):
    shapes = (
        jax.ShapeDtypeStruct((768, 256), BF16),
        jax.ShapeDtypeStruct((ROW_BLOCKS, BLK, HD), BF16),
    )
    return call(gather_kernel, (scalars,), packs, shapes, [], 2, 100_000)


def keys_of(packs, flops=100_000):
    rows = sum(p.shape[0] // 192 * 128 for p in packs)
    return call(keys_kernel, (), packs, jax.ShapeDtypeStruct((rows, 256), BF16), [], 2, flops)


def project(where, arrays):
    shape = jax.ShapeDtypeStruct((4, 128, 256), F32)
    scratch = [pltpu.VMEM((8, 4, 64, 256), BF16), pltpu.VMEM((4, 256, 256), F32)]
    return call(project_kernel, (where,), arrays, (shape, shape), scratch, 6, 1_000_000_000)


def attend(scalars, arrays):
    scratch = [
        pltpu.VMEM((CHUNK + TOKENS, 256), BF16),
        pltpu.VMEM((ROW_BLOCKS, 128, 128), BF16),
        pltpu.VMEM((ROW_BLOCKS + 1, BLK, LANES), I32),
        pltpu.VMEM((ROW_BLOCKS + MOST_EXTRA, 3, BLK, CHUNK), F32),
        pltpu.VMEM((ROW_BLOCKS + 1, 4, BLK, LANES), F32),
        pltpu.VMEM((ROW_BLOCKS + 1, 4, BLK, LANES), F32),
        pltpu.VMEM((ROW_BLOCKS + 1, BLK, LANES), F32),
        pltpu.SMEM((NDOC,), I32),
        pltpu.SMEM((MOST_EXTRA + TOGETHER,), I32),
        pltpu.SMEM((MOST_EXTRA + TOGETHER,), I32),
    ]
    shape = jax.ShapeDtypeStruct((512, 128), BF16)
    return call(attend_kernel, scalars, arrays, shape, scratch, 27, 2_000_000_000)


def curvature(where, arrays):
    shape = jax.ShapeDtypeStruct((2048, 128), BF16)
    scratch = [pltpu.VMEM((4, 128, 256), BF16), pltpu.VMEM((4, 128, 512), F32)]
    return call(curvature_kernel, (where,), arrays, shape, scratch, 6, 600_000_000)


def shift(value, axis, size, step):
    return lax.ppermute(value, axis, [(i, (i + step) % size) for i in range(size)])


def swap(value):
    return shift(value, "c", 2, 1)


def shift_plane(value, step, first):
    pairs = []
    for i in range(4):
        for c in range(2):
            for j in range(4):
                along_y = (c == 0) == first
                ii, jj = (i, (j + step) % 4) if along_y else ((i + step) % 4, j)
                pairs.append(((i * 2 + c) * 4 + j, (ii * 2 + c) * 4 + jj))
    return lax.ppermute(value, ("x", "c", "kvh"), pairs)


def per_device(
    hidden, query_weight, probe_vector, key_rows, value_rows, upstream, lengths, block_order
):
    z = lax.axis_index("z")
    x = lax.axis_index("x")
    c = lax.axis_index("c")
    y = lax.axis_index("kvh")
    where = jnp.stack([z, x, c, y]).astype(I32)
    scalars = jnp.concatenate([where, block_order, lengths])

    *packs, keep, send = prepare(
        where,
        tuple(
            pltpu.with_memory_space_constraint(a, pltpu.HBM)
            for a in (hidden, query_weight, probe_vector, key_rows, value_rows, upstream)
        ),
    )
    base = jnp.concatenate([keep, swap(send)], axis=0)
    packs = [packs[0]] + [shift(packs[dx], "x", 4, dx) for dx in (1, 2, 3)]
    base, *packs = lax.optimization_barrier((base, *packs))
    mine, upstream_rows = gather(scalars, packs)
    right_1, left_1 = shift(mine, "z", 8, 1), shift(mine, "z", 8, 7)

    stack = [base] + [shift_plane(base, s, True) for s in (3, 1, 2)]
    right_b, left_b, *stack = lax.optimization_barrier((right_1, left_1, *stack))
    stack = jnp.stack(stack)
    hid_left, hid_right, hid_far = [shift_plane(stack, n, False) for n in (3, 1, 2)]
    right_2, left_2 = shift(right_1, "z", 8, 1), shift(left_1, "z", 8, 7)

    right_3, left_3 = shift(right_2, "z", 8, 1), shift(left_2, "z", 8, 7)
    swap_a = swap(keys_of((mine, right_b, left_b), 100000))

    far_r, far_l = shift(right_3[:384], "z", 8, 1), shift(left_3[384:], "z", 8, 7)
    swap_b = swap(keys_of((right_2, left_2, right_3, left_3)))
    pieces = (stack, hid_left, hid_right, hid_far)

    ring = (mine, right_1, left_1, right_2, left_2, right_3, left_3)
    keys_c = keys_of((far_r, far_l), 4000000000)
    far_r, far_l, keys_c = lax.optimization_barrier((far_r, far_l, keys_c))
    swap_c = swap(keys_c)
    qt_keep, qt_send = project(where, (*pieces, *ring, far_r, far_l))
    qt_received = swap(qt_send)
    second_own = attend(
        (scalars,),
        (
            qt_keep,
            qt_received,
            *ring,
            far_r,
            far_l,
            swap_a,
            swap_b,
            swap_c,
            upstream_rows,
        ),
    )
    second_other = swap(second_own)
    partial = curvature(where, (*pieces, second_own, second_other))
    shares = lax.all_to_all(partial, ("z", "x"), 0, 0, tiled=True)
    summed = jnp.sum(shares.reshape(8, 4, 64, 128).astype(F32), axis=0)
    return summed.transpose(1, 0, 2).reshape(64, 512)


def solution(mesh):
    fine = Mesh(mesh.devices.reshape(8, 4, 2, 4), ("z", "x", "c", "kvh"))
    ctx = ("z", "x", "c")
    split = P(ctx, "kvh")
    return jax.shard_map(
        per_device,
        mesh=fine,
        in_specs=(split,) * 6 + (P(), P()),
        out_specs=split,
        check_vma=False,
    )
```

```python
import math

import jax
import jax.numpy as jnp
from jax import lax
from jax.experimental import pallas as pl
from jax.experimental.pallas import tpu as pltpu
from jax.sharding import Mesh, PartitionSpec as P

HD = 128
BLK = 64
NDOC = 16
CHUNK = 512
LANES = 128
ROW_BLOCKS = 8
MOST_EXTRA = ROW_BLOCKS * 4
TOGETHER = 4
ORDER = 4
LENGTHS = ORDER + 128
SCALE = 1.0 / math.sqrt(HD)
LOG2E = 1.4426950408889634
TOKENS = 8192
BF16 = jnp.bfloat16
F32 = jnp.float32
I32 = jnp.int32


def prepare_kernel(
    where_ref,
    query_hbm,
    probe_hbm,
    key_hbm,
    value_hbm,
    upstream_hbm,
    pack0_ref,
    pack1_ref,
    pack2_ref,
    pack3_ref,
    query_ref,
    probe_ref,
    key_ref,
    value_ref,
    upstream_ref,
    sems,
):
    x = where_ref[1]
    copies = [
        pltpu.make_async_copy(src, dst, sems.at[i])
        for i, (src, dst) in enumerate(
            (
                (query_hbm, query_ref),
                (probe_hbm, probe_ref),
                (key_hbm, key_ref),
                (value_hbm, value_ref),
                (upstream_hbm, upstream_ref),
            )
        )
    ]
    for copy in copies:
        copy.start()
    for copy in copies:
        copy.wait()
    for dx, pack in enumerate((pack0_ref, pack1_ref, pack2_ref, pack3_ref)):
        columns = pl.ds(pl.multiple_of(lax.rem(x + dx, 4) * HD, HD), HD)
        pack[0:64, 0:128] = query_ref[:, columns]
        pack[0:64, 128:256] = probe_ref[:, columns]
        pack[64:192, 0:128] = key_ref[...]
        pack[64:192, 128:256] = value_ref[...]
        pack[192:256, 0:128] = upstream_ref[0:64, columns]
        pack[192:256, 128:256] = upstream_ref[64:128, columns]


def select_kernel(where_ref, own_ref, other_ref, base_ref):
    c = where_ref[2]
    low = lax.broadcasted_iota(I32, (128, 128), 1) < 64
    for rows, ref in ((slice(0, 128), own_ref), (slice(128, 256), other_ref)):
        for k in range(4):
            a = ref[:, 256 * k : 256 * k + 128].astype(F32)
            b = ref[:, 256 * k + 128 : 256 * k + 256].astype(F32)
            first = jnp.where(low, a, pltpu.roll(b, 64, 1))
            second = jnp.where(low, pltpu.roll(a, 64, 1), b)
            base_ref[rows, 128 * k : 128 * k + 128] = jnp.where(c == 0, first, second).astype(BF16)


PLACE = (0, 2, 3, 1)


def hidden_piece(refs, r, s):
    return refs[PLACE[r]][PLACE[s]]


def project_kernel(*refs):
    where_ref, hidden = refs[0], refs[1:5]
    packs, far_r, far_l = refs[5:12], refs[12], refs[13]
    keep_ref, send_ref, weights = refs[14:]
    z, x, c, y = where_ref[0], where_ref[1], where_ref[2], where_ref[3]

    def place(pack, dz, places=(0, 1, 2, 3)):
        for i, dx in enumerate(places):
            weights[lax.rem(z - dz + 8, 8), lax.rem(x - dx + 4, 4)] = pack[
                i * 192 : i * 192 + 64, :
            ]

    for pack, dz in zip(packs, (0, 1, 7, 2, 6, 3, 5)):
        place(pack, dz)
    place(far_r, 4, (0, 1))
    place(far_l, 4, (2, 3))

    def products(piece):
        rows = []
        for dy in range(4):
            group = lax.rem(y - dy + 4, 4)
            rows.append(weights[pl.ds(group * 2, 2)].reshape(512, 256))
        w = jnp.concatenate(rows, axis=0)
        for dx in range(4):
            tokens = jnp.concatenate([piece(dx, dy) for dy in range(4)], axis=1)
            total = jnp.dot(tokens, w, preferred_element_type=F32)
            keep_ref[dx] = total[0:128]
            send_ref[dx] = total[128:256]

    @pl.when(c == 0)
    def _():
        products(lambda dx, dy: hidden_piece(hidden, dx, dy))

    @pl.when(c == 1)
    def _():
        products(lambda dx, dy: hidden_piece(hidden, dy, dx))


def attend_kernel(*refs):
    where_ref, qt_keep, qt_received = refs[:3]
    packs, far_r, far_l = refs[3:10], refs[10], refs[11]
    swap_a, swap_b, swap_c = refs[12:15]
    upstream_ref, second_ref = refs[15:17]
    (
        keys_values,
        query_tangent,
        starts,
        scores,
        sums,
        stats,
        second,
        ends,
        extra_block,
        extra_row,
    ) = refs[17:]
    z, x, c = where_ref[0], where_ref[1], where_ref[2]

    keys_values[0:CHUNK, :] = jnp.zeros((CHUNK, 256), BF16)

    def place(src, first_row, step, dz, cc, places=(0, 1, 2, 3)):
        zz = lax.rem(z - dz + 8, 8)
        for i, dx in enumerate(places):
            block = ((zz * 4 + lax.rem(x - dx + 4, 4)) * 2 + cc) * 2
            for b in range(2):
                target = pl.multiple_of(CHUNK + where_ref[ORDER + block + b] * BLK, BLK)
                row = first_row + i * step + b * 64
                keys_values[pl.ds(target, BLK), :] = src[row : row + 64, :]

    for pack, dz in zip(packs, (0, 1, 7, 2, 6, 3, 5)):
        place(pack, 64, 192, dz, c)
    place(far_r, 64, 192, 4, c, (0, 1))
    place(far_l, 64, 192, 4, c, (2, 3))
    for i, dz in enumerate((0, 1, 7)):
        place(swap_a, i * 512, 128, dz, 1 - c)
    for i, dz in enumerate((2, 6, 3, 5)):
        place(swap_b, i * 512, 128, dz, 1 - c)
    place(swap_c, 0, 128, 4, 1 - c)

    for rb in range(ROW_BLOCKS):
        rows = slice((rb % 2) * 64, (rb % 2) * 64 + 64)
        both = (qt_keep[rb // 2, rows, :] + qt_received[rb // 2, rows, :]).astype(BF16)
        query_tangent[rb, 0:64, :] = both[:, 0:128]
        query_tangent[rb, 64:128, :] = both[:, 128:256]

    total = jnp.int32(0)
    for d in range(NDOC):
        total = total + where_ref[LENGTHS + d]
        ends[d] = total
    packed_block = []
    extras = jnp.int32(0)
    sub = lax.broadcasted_iota(I32, (BLK, LANES), 0)
    lane = lax.broadcasted_iota(I32, (BLK, LANES), 1)
    for rb in range(ROW_BLOCKS):
        xx = lax.rem(x - rb // 2 + 4, 4)
        p = where_ref[ORDER + ((z * 4 + xx) * 2 + c) * 2 + rb % 2]
        packed_block.append(p)
        first = jnp.int32(0)
        start = jnp.zeros((BLK, LANES), I32)
        for d in range(NDOC):
            end = ends[d]
            first = jnp.where(end <= p * BLK, end, first)
            start = jnp.where(end <= p * BLK + sub, end, start)
        starts[rb] = start
        more = (p * BLK + BLK - first + CHUNK - 1) // CHUNK - 1

        def note(j, at, rb=rb, p=p):
            extra_block[at] = rb
            extra_row[at] = p * BLK + BLK - CHUNK * (j + 1)
            return at + 1

        extras = lax.fori_loop(0, more, note, extras)
    for n in range(TOGETHER - 1):
        extra_block[extras + n] = ROW_BLOCKS
        extra_row[extras + n] = 0
    sums[ROW_BLOCKS] = jnp.zeros((4, BLK, LANES), F32)
    stats[ROW_BLOCKS] = jnp.zeros((4, BLK, LANES), F32)
    second[ROW_BLOCKS] = jnp.zeros((BLK, LANES), F32)
    starts[ROW_BLOCKS] = jnp.zeros((BLK, LANES), I32)

    def dot_t(a, b):
        return lax.dot_general(a, b, (((1,), (1,)), ((), ())), preferred_element_type=F32)

    def scored(rb, source, row, last_pos):
        kv = keys_values[pl.ds(pl.multiple_of(row, BLK), CHUNK), :]
        st = dot_t(query_tangent[source], kv[:, 0:128])
        v = dot_t(upstream_ref[source], kv[:, 128:256])
        start = starts[rb]
        parts = []
        for i in range(CHUNK // LANES):
            cut = slice(i * LANES, (i + 1) * LANES)
            key_pos = row - CHUNK + i * LANES + lane
            allowed = key_pos >= start
            if last_pos is not None:
                allowed = allowed & (key_pos <= last_pos)
            e = jnp.where(allowed, jnp.exp2(st[0:64, cut] * (SCALE * LOG2E)), 0.0)
            parts.append((e, st[64:128, cut], v[:, cut]))
        return parts

    def row_sums(parts):
        out = [None] * 4
        for e, t, v in parts:
            ev = e * v
            for n, term in enumerate((e, ev, e * t, ev * t)):
                out[n] = term if out[n] is None else out[n] + term
        return out

    def keep_scores(slot, parts):
        for i, part in enumerate(parts):
            for n in range(3):
                scores[slot, n, :, i * LANES : (i + 1) * LANES] = part[n]

    def kept_scores(slot):
        cuts = [slice(i * LANES, (i + 1) * LANES) for i in range(CHUNK // LANES)]
        return [[scores[slot, n, :, cut] for n in range(3)] for cut in cuts]

    def weighted(rb, row, parts):
        value_mean, tangent_mean, drift, inverse = [stats[rb, n] for n in range(4)]
        pieces = []
        for e, t, v in parts:
            w = (e * inverse) * ((t - tangent_mean) * (v - value_mean) - drift)
            pieces.append(w.astype(BF16))
        keys = keys_values[pl.ds(pl.multiple_of(row, BLK), CHUNK), 0:128]
        return jnp.dot(jnp.concatenate(pieces, axis=1), keys, preferred_element_type=F32)

    for rb in range(ROW_BLOCKS):
        p = packed_block[rb]
        parts = scored(rb, rb, p * BLK + BLK, p * BLK + sub)
        keep_scores(rb, parts)
        for n, total in enumerate(row_sums(parts)):
            sums[rb, n] = total

    rounds = (extras + TOGETHER - 1) // TOGETHER

    def extra_scores(i, carry):
        for item in [TOGETHER * i + n for n in range(TOGETHER)]:
            rb = extra_block[item]
            parts = scored(rb, jnp.minimum(rb, ROW_BLOCKS - 1), extra_row[item], None)
            keep_scores(ROW_BLOCKS + item, parts)
            for n, total in enumerate(row_sums(parts)):
                sums[rb, n] += total
        return carry

    lax.fori_loop(0, rounds, extra_scores, 0)

    for rb in range(ROW_BLOCKS):
        weight_sum, value_sum, tangent_sum, joint_sum = [
            jnp.sum(sums[rb, n], axis=1, keepdims=True) for n in range(4)
        ]
        inverse = 1.0 / weight_sum
        value_mean = value_sum * inverse
        tangent_mean = tangent_sum * inverse
        drift = joint_sum * inverse - tangent_mean * value_mean
        for n, stat in enumerate((value_mean, tangent_mean, drift, inverse)):
            stats[rb, n] = jnp.broadcast_to(stat, (BLK, LANES))
    for rb in range(ROW_BLOCKS):
        second[rb] = weighted(rb, packed_block[rb] * BLK + BLK, kept_scores(rb))

    def extra_weights(i, carry):
        for item in [TOGETHER * i + n for n in range(TOGETHER)]:
            rb = extra_block[item]
            row = extra_row[item]
            second[rb] += weighted(rb, row, kept_scores(ROW_BLOCKS + item))
        return carry

    lax.fori_loop(0, rounds, extra_weights, 0)

    second_ref[...] = (
        second[0:ROW_BLOCKS].reshape(512, 128) * (SCALE * SCALE)
    ).astype(BF16)


def curvature_kernel(*refs):
    where_ref, hidden = refs[0], refs[1:5]
    second_own, second_other, out_ref, second_t = refs[5:]
    c, y = where_ref[2], where_ref[3]
    for dx in range(4):
        rows = slice(dx * 128, dx * 128 + 128)
        both = jnp.concatenate([second_own[rows, :], second_other[rows, :]], axis=0)
        second_t[:, dx * 256 : dx * 256 + 256] = both.astype(F32).T.astype(BF16)

    def products(piece):
        for dy in range(4):
            tokens = jnp.concatenate([piece(dx, dy) for dx in range(4)], axis=0)
            out = jnp.dot(second_t[...], tokens, preferred_element_type=F32)
            first = pl.multiple_of(lax.rem(y - dy + 4, 4) * 512, 512)
            out_ref[pl.ds(first, 512), :] = out.T.astype(BF16)

    @pl.when(c == 0)
    def _():
        products(lambda dx, dy: hidden_piece(hidden, dx, dy))

    @pl.when(c == 1)
    def _():
        products(lambda dx, dy: hidden_piece(hidden, dy, dx))


def gather_kernel(*refs):
    packs, (mine_ref, upstream_ref) = refs[1:5], refs[5:]
    for dx, pack in zip((0, 2, 1, 3), packs):
        mine_ref[dx * 192 : dx * 192 + 192, :] = pack[0:192, :]
        upstream_ref[2 * dx] = pack[192:256, 0:128]
        upstream_ref[2 * dx + 1] = pack[192:256, 128:256]


def keys_kernel(*refs):
    packs, out_ref = refs[:-1], refs[-1]
    at = 0
    for pack in packs:
        for dx in range(pack.shape[0] // 192):
            out_ref[at : at + 128, :] = pack[dx * 192 + 64 : dx * 192 + 192, :]
            at += 128


SMEM_SPEC = pl.BlockSpec(memory_space=pltpu.SMEM)
VMEM_SPEC = pl.BlockSpec(memory_space=pltpu.VMEM)


def call(kernel, scalars, arrays, out_shape, scratch, mebibytes, flops):
    return pl.pallas_call(
        kernel,
        out_shape=out_shape,
        in_specs=[SMEM_SPEC] * len(scalars) + [VMEM_SPEC] * len(arrays),
        out_specs=jax.tree.map(lambda _: VMEM_SPEC, out_shape),
        scratch_shapes=scratch,
        compiler_params=pltpu.CompilerParams(vmem_limit_bytes=mebibytes * 1024 * 1024),
        cost_estimate=pl.CostEstimate(flops=flops, bytes_accessed=8_000_000, transcendentals=0),
    )(*scalars, *arrays)


def prepare(where, arrays):
    any_spec = pl.BlockSpec(memory_space=pl.ANY)
    pack = jax.ShapeDtypeStruct((256, 256), BF16)
    return pl.pallas_call(
        prepare_kernel,
        out_shape=(pack,) * 4,
        in_specs=[SMEM_SPEC] + [any_spec] * 5,
        out_specs=(VMEM_SPEC,) * 4,
        scratch_shapes=[pltpu.VMEM(a.shape, BF16) for a in arrays]
        + [pltpu.SemaphoreType.DMA((5,))],
        compiler_params=pltpu.CompilerParams(vmem_limit_bytes=2 * 1024 * 1024),
        cost_estimate=pl.CostEstimate(flops=1_000_000, bytes_accessed=600_000, transcendentals=0),
    )(where, *arrays)


def gather(scalars, packs):
    shapes = (
        jax.ShapeDtypeStruct((768, 256), BF16),
        jax.ShapeDtypeStruct((ROW_BLOCKS, BLK, HD), BF16),
    )
    return call(gather_kernel, (scalars,), packs, shapes, [], 2, 100_000)


def keys_of(packs, flops=100_000):
    rows = sum(p.shape[0] // 192 * 128 for p in packs)
    return call(keys_kernel, (), packs, jax.ShapeDtypeStruct((rows, 256), BF16), [], 2, flops)


def select(where, arrays):
    shape = jax.ShapeDtypeStruct((256, 512), BF16)
    return call(select_kernel, (where,), arrays, shape, [], 2, 1_000_000)


def project(where, arrays):
    shape = jax.ShapeDtypeStruct((4, 128, 256), F32)
    scratch = [pltpu.VMEM((8, 4, 64, 256), BF16)]
    return call(project_kernel, (where,), arrays, (shape, shape), scratch, 8, 1_000_000_000)


def attend(scalars, arrays):
    scratch = [
        pltpu.VMEM((CHUNK + TOKENS, 256), BF16),
        pltpu.VMEM((ROW_BLOCKS, 128, 128), BF16),
        pltpu.VMEM((ROW_BLOCKS + 1, BLK, LANES), I32),
        pltpu.VMEM((ROW_BLOCKS + MOST_EXTRA, 3, BLK, CHUNK), F32),
        pltpu.VMEM((ROW_BLOCKS + 1, 4, BLK, LANES), F32),
        pltpu.VMEM((ROW_BLOCKS + 1, 4, BLK, LANES), F32),
        pltpu.VMEM((ROW_BLOCKS + 1, BLK, LANES), F32),
        pltpu.SMEM((NDOC,), I32),
        pltpu.SMEM((MOST_EXTRA + TOGETHER,), I32),
        pltpu.SMEM((MOST_EXTRA + TOGETHER,), I32),
    ]
    shape = jax.ShapeDtypeStruct((512, 128), BF16)
    return call(attend_kernel, scalars, arrays, shape, scratch, 27, 2_000_000_000)


def curvature(where, arrays):
    shape = jax.ShapeDtypeStruct((2048, 128), BF16)
    scratch = [pltpu.VMEM((128, 1024), BF16)]
    return call(curvature_kernel, (where,), arrays, shape, scratch, 8, 600_000_000)


def shift(value, axis, size, step):
    return lax.ppermute(value, axis, [(i, (i + step) % size) for i in range(size)])


def swap(value):
    return shift(value, "c", 2, 1)


def shift_plane(value, step, first):
    pairs = []
    for i in range(4):
        for c in range(2):
            for j in range(4):
                along_y = (c == 0) == first
                ii, jj = (i, (j + step) % 4) if along_y else ((i + step) % 4, j)
                pairs.append(((i * 2 + c) * 4 + j, (ii * 2 + c) * 4 + jj))
    return lax.ppermute(value, ("x", "c", "kvh"), pairs)


def per_device(
    hidden, query_weight, probe_vector, key_rows, value_rows, upstream, lengths, block_order
):
    z = lax.axis_index("z")
    x = lax.axis_index("x")
    c = lax.axis_index("c")
    y = lax.axis_index("kvh")
    where = jnp.stack([z, x, c, y]).astype(I32)
    scalars = jnp.concatenate([where, block_order, lengths])

    hidden_other = swap(hidden)
    packs = prepare(
        where,
        tuple(
            pltpu.with_memory_space_constraint(a, pltpu.HBM)
            for a in (query_weight, probe_vector, key_rows, value_rows, upstream)
        ),
    )
    base = select(where, (hidden, hidden_other))
    packs = [packs[0]] + [shift(packs[dx], "x", 4, dx) for dx in (2, 1, 3)]
    base, *packs = lax.optimization_barrier((base, *packs))
    mine, upstream_rows = gather(scalars, packs)
    right_1, left_1 = shift(mine, "z", 8, 1), shift(mine, "z", 8, 7)

    stack = [base] + [shift_plane(base, s, True) for s in (3, 1, 2)]
    right_b, left_b, *stack = lax.optimization_barrier((right_1, left_1, *stack))
    stack = jnp.stack(stack)
    hid_left, hid_right, hid_far = [shift_plane(stack, n, False) for n in (3, 1, 2)]
    right_2, left_2 = shift(right_1, "z", 8, 1), shift(left_1, "z", 8, 7)

    right_3, left_3 = shift(right_2, "z", 8, 1), shift(left_2, "z", 8, 7)
    swap_a = swap(keys_of((mine, right_b, left_b), 100000))

    far_r, far_l = shift(right_3[:384], "z", 8, 1), shift(left_3[384:], "z", 8, 7)
    swap_b = swap(keys_of((right_2, left_2, right_3, left_3)))
    pieces = (stack, hid_left, hid_right, hid_far)

    ring = (mine, right_1, left_1, right_2, left_2, right_3, left_3)
    keys_c = keys_of((far_r, far_l), 4000000000)
    far_r, far_l, keys_c = lax.optimization_barrier((far_r, far_l, keys_c))
    swap_c = swap(keys_c)
    qt_keep, qt_send = project(where, (*pieces, *ring, far_r, far_l))
    qt_received = swap(qt_send)
    second_own = attend(
        (scalars,),
        (
            qt_keep,
            qt_received,
            *ring,
            far_r,
            far_l,
            swap_a,
            swap_b,
            swap_c,
            upstream_rows,
        ),
    )
    second_other = swap(second_own)
    partial = curvature(where, (*pieces, second_own, second_other))
    shares = lax.all_to_all(partial, ("z", "x"), 0, 0, tiled=True)
    summed = jnp.sum(shares.reshape(8, 4, 64, 128).astype(F32), axis=0)
    return summed.transpose(1, 0, 2).reshape(64, 512)


def solution(mesh):
    fine = Mesh(mesh.devices.reshape(8, 4, 2, 4), ("z", "x", "c", "kvh"))
    ctx = ("z", "x", "c")
    split = P(ctx, "kvh")
    return jax.shard_map(
        per_device,
        mesh=fine,
        in_specs=(split,) * 6 + (P(), P()),
        out_specs=split,
        check_vma=False,
    )
```

```python
import math

import jax
import jax.numpy as jnp
from jax import lax
from jax.experimental import pallas as pl
from jax.experimental.pallas import tpu as pltpu
from jax.sharding import Mesh, PartitionSpec as P

HD = 128
BLK = 64
NDOC = 16
CHUNK = 512
LANES = 128
ROW_BLOCKS = 8
MOST_EXTRA = ROW_BLOCKS * 4
TOGETHER = 4
ORDER = 4
LENGTHS = ORDER + 128
SCALE = 1.0 / math.sqrt(HD)
LOG2E = 1.4426950408889634
TOKENS = 8192
BF16 = jnp.bfloat16
F32 = jnp.float32
I32 = jnp.int32


def prepare_kernel(
    where_ref,
    query_hbm,
    probe_hbm,
    key_hbm,
    value_hbm,
    upstream_hbm,
    pack0_ref,
    pack1_ref,
    pack2_ref,
    pack3_ref,
    query_ref,
    probe_ref,
    key_ref,
    value_ref,
    upstream_ref,
    sems,
):
    x = where_ref[1]
    copies = [
        pltpu.make_async_copy(src, dst, sems.at[i])
        for i, (src, dst) in enumerate(
            (
                (query_hbm, query_ref),
                (probe_hbm, probe_ref),
                (key_hbm, key_ref),
                (value_hbm, value_ref),
                (upstream_hbm, upstream_ref),
            )
        )
    ]
    for copy in copies:
        copy.start()
    for copy in copies:
        copy.wait()
    for dx, pack in enumerate((pack0_ref, pack1_ref, pack2_ref, pack3_ref)):
        columns = pl.ds(pl.multiple_of(lax.rem(x + dx, 4) * HD, HD), HD)
        pack[0:64, 0:128] = query_ref[:, columns]
        pack[0:64, 128:256] = probe_ref[:, columns]
        pack[64:192, 0:128] = key_ref[...]
        pack[64:192, 128:256] = value_ref[...]
        pack[192:256, 0:128] = upstream_ref[0:64, columns]
        pack[192:256, 128:256] = upstream_ref[64:128, columns]


def select_kernel(where_ref, own_ref, other_ref, base_ref):
    c = where_ref[2]
    low = lax.broadcasted_iota(I32, (128, 128), 1) < 64
    for rows, ref in ((slice(0, 128), own_ref), (slice(128, 256), other_ref)):
        for k in range(4):
            a = ref[:, 256 * k : 256 * k + 128].astype(F32)
            b = ref[:, 256 * k + 128 : 256 * k + 256].astype(F32)
            first = jnp.where(low, a, pltpu.roll(b, 64, 1))
            second = jnp.where(low, pltpu.roll(a, 64, 1), b)
            base_ref[rows, 128 * k : 128 * k + 128] = jnp.where(c == 0, first, second).astype(BF16)


PLACE = (0, 2, 3, 1)


def hidden_piece(refs, r, s):
    return refs[PLACE[r]][PLACE[s]]


def project_kernel(*refs):
    where_ref, hidden = refs[0], refs[1:5]
    packs, far_r, far_l = refs[5:12], refs[12], refs[13]
    keep_ref, send_ref, weights = refs[14:]
    z, x, c, y = where_ref[0], where_ref[1], where_ref[2], where_ref[3]

    def place(pack, dz, places=(0, 1, 2, 3)):
        for i, dx in enumerate(places):
            weights[lax.rem(z - dz + 8, 8), lax.rem(x - dx + 4, 4)] = pack[
                i * 192 : i * 192 + 64, :
            ]

    for pack, dz in zip(packs, (0, 1, 7, 2, 6, 3, 5)):
        place(pack, dz)
    place(far_r, 4, (0, 1, 2))
    place(far_l, 4, (3,))

    def products(piece):
        rows = []
        for dy in range(4):
            group = lax.rem(y - dy + 4, 4)
            rows.append(weights[pl.ds(group * 2, 2)].reshape(512, 256))
        w = jnp.concatenate(rows, axis=0)
        for dx in range(4):
            tokens = jnp.concatenate([piece(dx, dy) for dy in range(4)], axis=1)
            total = jnp.dot(tokens, w, preferred_element_type=F32)
            keep_ref[dx] = total[0:128]
            send_ref[dx] = total[128:256]

    @pl.when(c == 0)
    def _():
        products(lambda dx, dy: hidden_piece(hidden, dx, dy))

    @pl.when(c == 1)
    def _():
        products(lambda dx, dy: hidden_piece(hidden, dy, dx))


def plan_kernel(where_ref, starts, extra_block, extra_row, ends):
    z, x, c = where_ref[0], where_ref[1], where_ref[2]
    total = jnp.int32(0)
    for d in range(NDOC):
        total = total + where_ref[LENGTHS + d]
        ends[d] = total
    extras = jnp.int32(0)
    sub = lax.broadcasted_iota(I32, (BLK, LANES), 0)
    for rb in range(ROW_BLOCKS):
        xx = lax.rem(x - rb // 2 + 4, 4)
        p = where_ref[ORDER + ((z * 4 + xx) * 2 + c) * 2 + rb % 2]
        first = jnp.int32(0)
        start = jnp.zeros((BLK, LANES), I32)
        for d in range(NDOC):
            end = ends[d]
            first = jnp.where(end <= p * BLK, end, first)
            start = jnp.where(end <= p * BLK + sub, end, start)
        starts[rb] = start
        more = (p * BLK + BLK - first + CHUNK - 1) // CHUNK - 1

        def note(j, at, rb=rb, p=p):
            extra_block[at] = rb
            extra_row[at] = p * BLK + BLK - CHUNK * (j + 1)
            return at + 1

        extras = lax.fori_loop(0, more, note, extras)
    for n in range(TOGETHER - 1):
        extra_block[extras + n] = ROW_BLOCKS
        extra_row[extras + n] = 0
    extra_block[MOST_EXTRA + TOGETHER] = extras
    starts[ROW_BLOCKS] = jnp.zeros((BLK, LANES), I32)


def attend_kernel(*refs):
    where_ref, extra_block, extra_row, qt_keep, qt_received = refs[:5]
    packs, far_r, far_l = refs[5:12], refs[12], refs[13]
    swap_a, swap_b, swap_c = refs[14:17]
    upstream_ref, starts, second_ref = refs[17:20]
    (
        keys_values,
        query_tangent,
        scores,
        sums,
        stats,
        second,
    ) = refs[20:]
    z, x, c = where_ref[0], where_ref[1], where_ref[2]

    keys_values[0:CHUNK, :] = jnp.zeros((CHUNK, 256), BF16)

    def place(src, first_row, step, dz, cc, places=(0, 1, 2, 3)):
        zz = lax.rem(z - dz + 8, 8)
        for i, dx in enumerate(places):
            block = ((zz * 4 + lax.rem(x - dx + 4, 4)) * 2 + cc) * 2
            for b in range(2):
                target = pl.multiple_of(CHUNK + where_ref[ORDER + block + b] * BLK, BLK)
                row = first_row + i * step + b * 64
                keys_values[pl.ds(target, BLK), :] = src[row : row + 64, :]

    for pack, dz in zip(packs, (0, 1, 7, 2, 6, 3, 5)):
        place(pack, 64, 192, dz, c)
    place(far_r, 64, 192, 4, c, (0, 1, 2))
    place(far_l, 64, 192, 4, c, (3,))
    for i, dz in enumerate((0, 1, 7)):
        place(swap_a, i * 512, 128, dz, 1 - c)
    for i, dz in enumerate((2, 6, 3, 5)):
        place(swap_b, i * 512, 128, dz, 1 - c)
    place(swap_c, 0, 128, 4, 1 - c)

    for rb in range(ROW_BLOCKS):
        rows = slice((rb % 2) * 64, (rb % 2) * 64 + 64)
        both = (qt_keep[rb // 2, rows, :] + qt_received[rb // 2, rows, :]).astype(BF16)
        query_tangent[rb, 0:64, :] = both[:, 0:128]
        query_tangent[rb, 64:128, :] = both[:, 128:256]

    packed_block = []
    for rb in range(ROW_BLOCKS):
        xx = lax.rem(x - rb // 2 + 4, 4)
        packed_block.append(where_ref[ORDER + ((z * 4 + xx) * 2 + c) * 2 + rb % 2])
    extras = extra_block[MOST_EXTRA + TOGETHER]
    sub = lax.broadcasted_iota(I32, (BLK, LANES), 0)
    lane = lax.broadcasted_iota(I32, (BLK, LANES), 1)
    sums[ROW_BLOCKS] = jnp.zeros((4, BLK, LANES), F32)
    stats[ROW_BLOCKS] = jnp.zeros((4, BLK, LANES), F32)
    second[ROW_BLOCKS] = jnp.zeros((BLK, LANES), F32)

    def dot_t(a, b):
        return lax.dot_general(a, b, (((1,), (1,)), ((), ())), preferred_element_type=F32)

    def scored(rb, source, row, last_pos):
        kv = keys_values[pl.ds(pl.multiple_of(row, BLK), CHUNK), :]
        st = dot_t(query_tangent[source], kv[:, 0:128])
        v = dot_t(upstream_ref[source], kv[:, 128:256])
        start = starts[rb]
        parts = []
        for i in range(CHUNK // LANES):
            cut = slice(i * LANES, (i + 1) * LANES)
            key_pos = row - CHUNK + i * LANES + lane
            allowed = key_pos >= start
            if last_pos is not None:
                allowed = allowed & (key_pos <= last_pos)
            e = jnp.where(allowed, jnp.exp2(st[0:64, cut] * (SCALE * LOG2E)), 0.0)
            parts.append((e, st[64:128, cut], v[:, cut]))
        return parts

    def row_sums(parts):
        out = [None] * 4
        for e, t, v in parts:
            ev = e * v
            for n, term in enumerate((e, ev, e * t, ev * t)):
                out[n] = term if out[n] is None else out[n] + term
        return out

    def keep_scores(slot, parts):
        for i, part in enumerate(parts):
            for n in range(3):
                scores[slot, n, :, i * LANES : (i + 1) * LANES] = part[n]

    def kept_scores(slot):
        cuts = [slice(i * LANES, (i + 1) * LANES) for i in range(CHUNK // LANES)]
        return [[scores[slot, n, :, cut] for n in range(3)] for cut in cuts]

    def weighted(rb, row, parts):
        value_mean, tangent_mean, drift, inverse = [stats[rb, n] for n in range(4)]
        pieces = []
        for e, t, v in parts:
            w = (e * inverse) * ((t - tangent_mean) * (v - value_mean) - drift)
            pieces.append(w.astype(BF16))
        keys = keys_values[pl.ds(pl.multiple_of(row, BLK), CHUNK), 0:128]
        return jnp.dot(jnp.concatenate(pieces, axis=1), keys, preferred_element_type=F32)

    for rb in range(ROW_BLOCKS):
        p = packed_block[rb]
        parts = scored(rb, rb, p * BLK + BLK, p * BLK + sub)
        keep_scores(rb, parts)
        for n, total in enumerate(row_sums(parts)):
            sums[rb, n] = total

    rounds = (extras + TOGETHER - 1) // TOGETHER

    def extra_scores(i, carry):
        for item in [TOGETHER * i + n for n in range(TOGETHER)]:
            rb = extra_block[item]
            parts = scored(rb, jnp.minimum(rb, ROW_BLOCKS - 1), extra_row[item], None)
            keep_scores(ROW_BLOCKS + item, parts)
            for n, total in enumerate(row_sums(parts)):
                sums[rb, n] += total
        return carry

    lax.fori_loop(0, rounds, extra_scores, 0)

    for rb in range(ROW_BLOCKS):
        weight_sum, value_sum, tangent_sum, joint_sum = [
            jnp.sum(sums[rb, n], axis=1, keepdims=True) for n in range(4)
        ]
        inverse = 1.0 / weight_sum
        value_mean = value_sum * inverse
        tangent_mean = tangent_sum * inverse
        drift = joint_sum * inverse - tangent_mean * value_mean
        for n, stat in enumerate((value_mean, tangent_mean, drift, inverse)):
            stats[rb, n] = jnp.broadcast_to(stat, (BLK, LANES))
    for rb in range(ROW_BLOCKS):
        second[rb] = weighted(rb, packed_block[rb] * BLK + BLK, kept_scores(rb))

    def extra_weights(i, carry):
        for item in [TOGETHER * i + n for n in range(TOGETHER)]:
            rb = extra_block[item]
            row = extra_row[item]
            second[rb] += weighted(rb, row, kept_scores(ROW_BLOCKS + item))
        return carry

    lax.fori_loop(0, rounds, extra_weights, 0)

    second_ref[...] = (
        second[0:ROW_BLOCKS].reshape(512, 128) * (SCALE * SCALE)
    ).astype(BF16)


def curvature_kernel(*refs):
    where_ref, hidden = refs[0], refs[1:5]
    second_own, second_other, out_ref, second_t = refs[5:]
    c, y = where_ref[2], where_ref[3]
    for dx in range(4):
        rows = slice(dx * 128, dx * 128 + 128)
        both = jnp.concatenate([second_own[rows, :], second_other[rows, :]], axis=0)
        second_t[:, dx * 256 : dx * 256 + 256] = both.astype(F32).T.astype(BF16)

    def products(piece):
        for dy in range(4):
            tokens = jnp.concatenate([piece(dx, dy) for dx in range(4)], axis=0)
            out = jnp.dot(second_t[...], tokens, preferred_element_type=F32)
            first = pl.multiple_of(lax.rem(y - dy + 4, 4) * 512, 512)
            out_ref[pl.ds(first, 512), :] = out.T.astype(BF16)

    @pl.when(c == 0)
    def _():
        products(lambda dx, dy: hidden_piece(hidden, dx, dy))

    @pl.when(c == 1)
    def _():
        products(lambda dx, dy: hidden_piece(hidden, dy, dx))


def gather_kernel(*refs):
    packs, (mine_ref, upstream_ref) = refs[2:6], refs[6:]
    for dx, pack in zip((0, 2, 1, 3), packs):
        mine_ref[dx * 192 : dx * 192 + 192, :] = pack[0:192, :]
        upstream_ref[2 * dx] = pack[192:256, 0:128]
        upstream_ref[2 * dx + 1] = pack[192:256, 128:256]


def keys_kernel(*refs):
    packs, out_ref = refs[:-1], refs[-1]
    at = 0
    for pack in packs:
        for dx in range(pack.shape[0] // 192):
            out_ref[at : at + 128, :] = pack[dx * 192 + 64 : dx * 192 + 192, :]
            at += 128


SMEM_SPEC = pl.BlockSpec(memory_space=pltpu.SMEM)
VMEM_SPEC = pl.BlockSpec(memory_space=pltpu.VMEM)


def call(kernel, scalars, arrays, out_shape, scratch, mebibytes, flops):
    return pl.pallas_call(
        kernel,
        out_shape=out_shape,
        in_specs=[SMEM_SPEC] * len(scalars) + [VMEM_SPEC] * len(arrays),
        out_specs=jax.tree.map(lambda _: VMEM_SPEC, out_shape),
        scratch_shapes=scratch,
        compiler_params=pltpu.CompilerParams(vmem_limit_bytes=mebibytes * 1024 * 1024),
        cost_estimate=pl.CostEstimate(flops=flops, bytes_accessed=8_000_000, transcendentals=0),
    )(*scalars, *arrays)


def prepare(where, arrays):
    any_spec = pl.BlockSpec(memory_space=pl.ANY)
    pack = jax.ShapeDtypeStruct((256, 256), BF16)
    return pl.pallas_call(
        prepare_kernel,
        out_shape=(pack,) * 4,
        in_specs=[SMEM_SPEC] + [any_spec] * 5,
        out_specs=(VMEM_SPEC,) * 4,
        scratch_shapes=[pltpu.VMEM(a.shape, BF16) for a in arrays]
        + [pltpu.SemaphoreType.DMA((5,))],
        compiler_params=pltpu.CompilerParams(vmem_limit_bytes=2 * 1024 * 1024),
        cost_estimate=pl.CostEstimate(flops=1_000_000, bytes_accessed=600_000, transcendentals=0),
    )(where, *arrays)


def gather(scalars, starts, packs):
    shapes = (
        jax.ShapeDtypeStruct((768, 256), BF16),
        jax.ShapeDtypeStruct((ROW_BLOCKS, BLK, HD), BF16),
    )
    return call(gather_kernel, (scalars,), (starts, *packs), shapes, [], 2, 100_000)


def keys_of(packs, flops=100_000):
    rows = sum(p.shape[0] // 192 * 128 for p in packs)
    return call(keys_kernel, (), packs, jax.ShapeDtypeStruct((rows, 256), BF16), [], 2, flops)


def select(where, arrays):
    shape = jax.ShapeDtypeStruct((256, 512), BF16)
    return call(select_kernel, (where,), arrays, shape, [], 2, 1_000_000)


def project(where, arrays):
    shape = jax.ShapeDtypeStruct((4, 128, 256), F32)
    scratch = [pltpu.VMEM((8, 4, 64, 256), BF16)]
    return call(project_kernel, (where,), arrays, (shape, shape), scratch, 8, 1_000_000_000)


def plan(scalars):
    items = jax.ShapeDtypeStruct((MOST_EXTRA + TOGETHER + 1,), I32)
    return pl.pallas_call(
        plan_kernel,
        out_shape=(jax.ShapeDtypeStruct((ROW_BLOCKS + 1, BLK, LANES), I32), items, items),
        in_specs=[SMEM_SPEC],
        out_specs=(VMEM_SPEC, SMEM_SPEC, SMEM_SPEC),
        scratch_shapes=[pltpu.SMEM((NDOC,), I32)],
        compiler_params=pltpu.CompilerParams(vmem_limit_bytes=2 * 1024 * 1024),
        cost_estimate=pl.CostEstimate(flops=100_000, bytes_accessed=300_000, transcendentals=0),
    )(scalars)


def attend(scalars, arrays):
    scratch = [
        pltpu.VMEM((CHUNK + TOKENS, 256), BF16),
        pltpu.VMEM((ROW_BLOCKS, 128, 128), BF16),
        pltpu.VMEM((ROW_BLOCKS + MOST_EXTRA, 3, BLK, CHUNK), F32),
        pltpu.VMEM((ROW_BLOCKS + 1, 4, BLK, LANES), F32),
        pltpu.VMEM((ROW_BLOCKS + 1, 4, BLK, LANES), F32),
        pltpu.VMEM((ROW_BLOCKS + 1, BLK, LANES), F32),
    ]
    shape = jax.ShapeDtypeStruct((512, 128), BF16)
    return call(attend_kernel, scalars, arrays, shape, scratch, 27, 2_000_000_000)


def curvature(where, arrays):
    shape = jax.ShapeDtypeStruct((2048, 128), BF16)
    scratch = [pltpu.VMEM((128, 1024), BF16)]
    return call(curvature_kernel, (where,), arrays, shape, scratch, 8, 600_000_000)


def shift(value, axis, size, step):
    return lax.ppermute(value, axis, [(i, (i + step) % size) for i in range(size)])


def swap(value):
    return shift(value, "c", 2, 1)


def shift_plane(value, step, first):
    pairs = []
    for i in range(4):
        for c in range(2):
            for j in range(4):
                along_y = (c == 0) == first
                ii, jj = (i, (j + step) % 4) if along_y else ((i + step) % 4, j)
                pairs.append(((i * 2 + c) * 4 + j, (ii * 2 + c) * 4 + jj))
    return lax.ppermute(value, ("x", "c", "kvh"), pairs)


def per_device(
    hidden, query_weight, probe_vector, key_rows, value_rows, upstream, lengths, block_order
):
    z = lax.axis_index("z")
    x = lax.axis_index("x")
    c = lax.axis_index("c")
    y = lax.axis_index("kvh")
    where = jnp.stack([z, x, c, y]).astype(I32)
    scalars = jnp.concatenate([where, block_order, lengths])

    hidden_other = swap(hidden)
    packs = prepare(
        where,
        tuple(
            pltpu.with_memory_space_constraint(a, pltpu.HBM)
            for a in (query_weight, probe_vector, key_rows, value_rows, upstream)
        ),
    )
    base = select(where, (hidden, hidden_other))
    packs = [packs[0]] + [shift(packs[dx], "x", 4, dx) for dx in (2, 1, 3)]
    base, *packs = lax.optimization_barrier((base, *packs))
    starts, extra_block, extra_row = plan(scalars)
    mine, upstream_rows = gather(scalars, starts, packs)
    right_1, left_1 = shift(mine, "z", 8, 1), shift(mine, "z", 8, 7)

    stack = [base] + [shift_plane(base, s, True) for s in (3, 1, 2)]
    right_b, left_b, *stack = lax.optimization_barrier((right_1, left_1, *stack))
    stack = jnp.stack(stack)
    hid_left, hid_right, hid_far = [shift_plane(stack, n, False) for n in (3, 1, 2)]
    right_2, left_2 = shift(right_1, "z", 8, 1), shift(left_1, "z", 8, 7)

    right_3, left_3 = shift(right_2, "z", 8, 1), shift(left_2, "z", 8, 7)
    swap_a = swap(keys_of((mine, right_b, left_b), 100000))

    far_r, far_l = shift(right_3[:576], "z", 8, 1), shift(left_3[576:], "z", 8, 7)
    swap_b = swap(keys_of((right_2, left_2, right_3, left_3)))
    pieces = (stack, hid_left, hid_right, hid_far)

    ring = (mine, right_1, left_1, right_2, left_2, right_3, left_3)
    keys_c = keys_of((far_r, far_l), 3000000000)
    far_r, far_l, keys_c = lax.optimization_barrier((far_r, far_l, keys_c))
    swap_c = swap(keys_c)
    qt_keep, qt_send = project(where, (*pieces, *ring, far_r, far_l))
    qt_received = swap(qt_send)
    second_own = attend(
        (scalars, extra_block, extra_row),
        (
            qt_keep,
            qt_received,
            *ring,
            far_r,
            far_l,
            swap_a,
            swap_b,
            swap_c,
            upstream_rows,
            starts,
        ),
    )
    second_other = swap(second_own)
    partial = curvature(where, (*pieces, second_own, second_other))
    shares = lax.all_to_all(partial, ("z", "x"), 0, 0, tiled=True)
    summed = jnp.sum(shares.reshape(8, 4, 64, 128).astype(F32), axis=0)
    return summed.transpose(1, 0, 2).reshape(64, 512)


def solution(mesh):
    fine = Mesh(mesh.devices.reshape(8, 4, 2, 4), ("z", "x", "c", "kvh"))
    ctx = ("z", "x", "c")
    split = P(ctx, "kvh")
    return jax.shard_map(
        per_device,
        mesh=fine,
        in_specs=(split,) * 6 + (P(), P()),
        out_specs=split,
        check_vma=False,
    )
```
